128 devices in a mesh: group: 4 (over z), ctx: 32 (over x, y, core).
Axes of the slice: x: 4, y: 4, z: 4, core: 2. Of those that a mesh axis runs over, the one named last changes fastest.
Arguments:
- hidden_states: bfloat16 [2, 32, 4096], P(None, 'group'), may hold values from -6 to 6
- key_values: bfloat16 [32, 16384, 1024], P('group', 'ctx'), may hold values from -128 to 128
- lengths: int32 [32], replicated, may hold values from 1 to 16384, as said below
- move_source: int32 [12], replicated, may hold values from 0 to 31, as said below
- move_target: int32 [12], replicated, may hold values from 0 to 31, as said below
- query_weight: bfloat16 [4096, 8192], P(None, 'ctx'), may hold values from -0.13125 to 0.13125
- keyval_weight: bfloat16 [4096, 1024], P(None, 'ctx'), may hold values from -0.09375 to 0.09375
- query_gain: bfloat16 [128], replicated, may hold values from 0.25 to 1.75
- key_gain: bfloat16 [128], replicated, may hold values from 0.25 to 1.75
- output_weight: bfloat16 [8192, 4096], P('ctx'), may hold values from -0.125 to 0.125
Outputs:
- attended: bfloat16 [2, 32, 4096], P(None, 'group', 'ctx')
The draws below stay inside these ranges and needn't reach their ends.
Inputs may be any that keep to these rules, and one draw needn't show every extreme that they name: `lengths`: some row holds exactly 16384 cached tokens. move_source lists distinct slots and move_target lists the same set of slots in another order; for every ordered pair of different groups exactly 1 entries have the source slot in the first group and the target slot in the second; group of a slot is slot // 8; rows of unlisted slots keep their slot. `move_target`: see move_source.
All inputs are finite; a program needn't handle non-finite values.
Results may differ from the reference program's by a relative error of at most 0.021.
Values may be sent and summed in bfloat16 or wider, within the bound.
A program may use at most 128 MiB of HBM per device.

```python
import math
import jax
import jax.numpy as jnp
import numpy as np
from jax import lax

D = 4096
HEADS = 64
KV_HEADS = 4
HEAD_DIM = 128
ROWS_GRP = 8
BLK = 512
MOVE = 1
STEPS = 2
ROWS_ALL = 32
CAP = 16384
N_CTX = 32


def shared_base(key):
    return jnp.clip(jax.random.normal(key, (D, KV_HEADS, HEAD_DIM), jnp.float32), -6.0, 6.0)


def draw_query_weight(key, part):
    base = shared_base(key)
    key = jax.random.fold_in(key, 3)
    fresh = jnp.clip(jax.random.normal(key, (D, HEADS, HEAD_DIM), jnp.float32), -6.0, 6.0)
    tied = jnp.repeat(base, HEADS // KV_HEADS, axis=1)
    mixed_weight = (0.8 * tied + 0.6 * fresh) / math.sqrt(D)
    return mixed_weight.reshape(D, HEADS * HEAD_DIM).astype(jnp.bfloat16)


def draw_keyval_weight(key, part):
    base = shared_base(key)
    key = jax.random.fold_in(key, 4)
    fresh = jnp.clip(jax.random.normal(key, (D, KV_HEADS * HEAD_DIM), jnp.float32), -6.0, 6.0)
    joined = jnp.concatenate([base.reshape(D, KV_HEADS * HEAD_DIM), fresh], axis=1) / math.sqrt(D)
    return joined.astype(jnp.bfloat16)


def draw_key_values(key, part):
    key = jax.random.fold_in(key, 5)
    noise_key = jax.random.fold_in(key, 0)
    shape = (ROWS_ALL, CAP, 2 * KV_HEADS * HEAD_DIM)
    return jnp.clip(jax.random.normal(noise_key, shape, jnp.float32), -6.0, 6.0).astype(jnp.bfloat16)


def draw_lengths(key, part):
    key = jax.random.fold_in(key, 7)
    main_key, tail_key, pick_key = jax.random.split(key, 3)
    drawn = jnp.maximum(jax.random.randint(main_key, (ROWS_ALL,), 1, CAP + 1), jax.random.randint(tail_key, (ROWS_ALL,), 1, CAP + 1))
    chosen = jax.random.randint(pick_key, (), 0, ROWS_ALL)
    return drawn.at[chosen].set(CAP).astype(jnp.int32)


def migration_lists(key):
    groups = ROWS_ALL // ROWS_GRP
    others = groups - 1
    keys = jax.random.split(key, groups + 1)
    leaving = jnp.stack([jax.random.permutation(keys[index], ROWS_GRP)[:MOVE * others] for index in range(groups)])
    src_group = []
    src_column = []
    dst_group = []
    dst_column = []
    for sender in range(groups):
        for taker in range(groups):
            if taker == sender:
                continue
            taker_place = taker if taker < sender else taker - 1
            sender_place = sender if sender < taker else sender - 1
            for rank_index in range(MOVE):
                src_group.append(sender)
                src_column.append(taker_place * MOVE + rank_index)
                dst_group.append(taker)
                dst_column.append(sender_place * MOVE + rank_index)
    src_group = np.array(src_group, np.int32)
    src_column = np.array(src_column, np.int32)
    dst_group = np.array(dst_group, np.int32)
    dst_column = np.array(dst_column, np.int32)
    source = src_group * ROWS_GRP + leaving[src_group, src_column]
    target = dst_group * ROWS_GRP + leaving[dst_group, dst_column]
    order = jax.random.permutation(keys[groups], source.shape[0])
    return (source[order].astype(jnp.int32), target[order].astype(jnp.int32))


def draw_move_source(key, part):
    source, target = migration_lists(key)
    return source


def draw_move_target(key, part):
    source, target = migration_lists(key)
    return target


def with_spikes(entries, rng, source, target, blocks, factor):
    def block_of(dim):
        return (jnp.arange(entries.shape[dim]) // (entries.shape[dim] // blocks)).reshape((-1,) + (1,) * (entries.ndim - 1 - dim))

    one_side = jax.random.permutation(rng, blocks)[block_of(target)]
    other_side = (block_of(target) + blocks // 2) % blocks
    return jnp.where((block_of(source) == one_side) | (block_of(source) == other_side), factor * entries, entries)


def block_scale(rng, extent, shards, low, high):
    loudness = 1.0
    for axis_at, blocks in shards:
        draws = jax.random.uniform(jax.random.fold_in(jax.random.fold_in(rng, 6), axis_at), (blocks,), jnp.float32, low / len(shards), high / len(shards))
        loudness = loudness * jnp.repeat(jnp.exp(draws), extent[axis_at] // blocks).reshape((-1,) + (1,) * (len(extent) - 1 - axis_at))
    return loudness


def scatter_about(rng, shape, deviation, reach, shards=(), kind=jnp.bfloat16):
    result = jax.random.normal(rng, shape, jnp.float32) * deviation
    if len(shards) > 0:
        result = block_scale(rng, shape, shards, -0.22, 0.18) * result
    return jnp.clip(result, min=-reach, max=reach).astype(kind)


def noise_with(own_key, shape, width, bound, shards, heavy, kind=jnp.bfloat16):
    values = width * jax.random.normal(own_key, shape, jnp.float32)
    if shards:
        values = values * block_scale(own_key, shape, shards, -0.22, 0.18)
    return jnp.clip(with_spikes(values, jax.random.fold_in(own_key, 3), *heavy), -bound, bound).astype(kind)


def setup_inputs(seed: int = 0) -> dict:
    streams_of = jax.random.split(jax.random.key(seed), 11)
    return {
        "hidden_states": scatter_about(streams_of[0], (STEPS, ROWS_ALL, D), 1.0, 6.0, ((1, 4),)),
        "key_values": draw_key_values(jax.random.fold_in(streams_of[10], 71), 0),
        "lengths": draw_lengths(jax.random.fold_in(streams_of[10], 71), 0),
        "move_source": draw_move_source(jax.random.fold_in(streams_of[10], 71), 0),
        "move_target": draw_move_target(jax.random.fold_in(streams_of[10], 71), 0),
        "query_weight": draw_query_weight(jax.random.fold_in(streams_of[10], 71), 0),
        "keyval_weight": draw_keyval_weight(jax.random.fold_in(streams_of[10], 71), 0),
        "query_gain": jnp.clip(1.0 + 0.15 * jax.random.normal(streams_of[7], (HEAD_DIM,), jnp.float32), 0.25, 1.75).astype(jnp.bfloat16),
        "key_gain": jnp.clip(1.0 + 0.15 * jax.random.normal(streams_of[8], (HEAD_DIM,), jnp.float32), 0.25, 1.75).astype(jnp.bfloat16),
        "output_weight": noise_with(streams_of[9], (HEADS * HEAD_DIM, D), (HEADS * HEAD_DIM) ** -0.5, 0.125, ((0, 32),), (0, 1, 32, 2.75)),
    }


eps = 1e-06
theta = 1000000.0
floor_value = -1e+30

def normed_rotated(values, gain_row, position):
    halfway = values.shape[-1] // 2
    scaled = values * lax.rsqrt(lax.optimization_barrier(jnp.mean(values * values, axis=-1, keepdims=True)) + eps) * gain_row.astype(jnp.float32)
    freqs = theta ** (-2.0 * jnp.arange(halfway, dtype=jnp.float32) / values.shape[-1])
    angles = position.astype(jnp.float32)[..., None, None] * freqs
    leading = scaled[..., :halfway]
    trailing = scaled[..., halfway:]
    cosine = jnp.cos(angles)
    sine_part = jnp.sin(angles)
    return jnp.concatenate([leading * cosine - trailing * sine_part, trailing * cosine + leading * sine_part], axis=-1)

def block_terms(scores, usable):
    masked = jnp.where(usable, scores, floor_value)
    highest = lax.optimization_barrier(jnp.max(masked, axis=-1))
    weights = jnp.where(usable, jnp.exp(masked - highest[..., None]), 0.0)
    rounded = lax.optimization_barrier(weights.astype(jnp.bfloat16)).astype(jnp.float32)
    return (highest, lax.optimization_barrier(jnp.sum(weights, axis=-1)), rounded)

def anchors(move_source, move_target):
    slots = jnp.arange(ROWS_ALL, dtype=jnp.int32)
    hits = move_target[None, :] == slots[:, None]
    moved = lax.optimization_barrier(jnp.sum(jnp.where(hits, move_source[None, :], 0), axis=1)).astype(jnp.int32)
    return jnp.where(jnp.any(hits, axis=1), moved, slots)

def reference(hidden_states, key_values, lengths, move_source, move_target, query_weight, keyval_weight, query_gain, key_gain, output_weight):
    anchor = anchors(move_source, move_target)
    row_lengths = lengths[anchor]
    flat_hidden = hidden_states.reshape(STEPS * ROWS_ALL, D)
    queries = jnp.dot(flat_hidden, query_weight, preferred_element_type=jnp.float32).astype(jnp.bfloat16)
    new_kv = jnp.dot(flat_hidden, keyval_weight, preferred_element_type=jnp.float32).astype(jnp.bfloat16)
    queries = queries.reshape(STEPS, ROWS_ALL, HEADS, HEAD_DIM)
    new_kv = new_kv.reshape(STEPS, ROWS_ALL, 2, KV_HEADS, HEAD_DIM)
    positions = row_lengths[None, :] + jnp.arange(STEPS, dtype=jnp.int32)[:, None]
    query_rot = normed_rotated(queries.astype(jnp.float32), query_gain, positions).astype(jnp.bfloat16)
    new_keys = normed_rotated(new_kv[:, :, 0].astype(jnp.float32), key_gain, positions).astype(jnp.bfloat16)
    new_values = new_kv[:, :, 1]
    score_scale = HEAD_DIM ** (-0.5)
    per_group = HEADS // KV_HEADS
    causal = (jnp.arange(STEPS)[None, :] <= jnp.arange(STEPS)[:, None]).reshape(STEPS, 1, 1, STEPS)

    def one_row(row_index):
        length = row_lengths[row_index]
        row_cache = key_values[anchor[row_index]]
        cache_keys = row_cache[:, :KV_HEADS * HEAD_DIM].reshape(N_CTX, BLK, KV_HEADS, HEAD_DIM).astype(jnp.float32)
        cache_vals = row_cache[:, KV_HEADS * HEAD_DIM:].reshape(N_CTX, BLK, KV_HEADS, HEAD_DIM).astype(jnp.float32)
        query_row = query_rot[:, row_index].reshape(STEPS, KV_HEADS, per_group, HEAD_DIM).astype(jnp.float32)
        scores = jnp.einsum('sgjd,cpgd->scgjp', query_row, cache_keys) * score_scale
        usable = (jnp.arange(CAP) < length).reshape(N_CTX, 1, 1, BLK)
        highest, totals, rounded = block_terms(scores, usable)
        sums = jnp.einsum('scgjp,cpgd->scgjd', rounded, cache_vals)
        key_row = new_keys[:, row_index].astype(jnp.float32)
        value_row = new_values[:, row_index].astype(jnp.float32)
        new_scores = jnp.einsum('sgjd,tgd->sgjt', query_row, key_row) * score_scale
        new_high, new_total, new_rounded = block_terms(new_scores, causal)
        new_sums = jnp.einsum('sgjt,tgd->sgjd', new_rounded, value_row)
        peak = jnp.maximum(lax.optimization_barrier(jnp.max(highest, axis=1)), new_high)
        cache_factor = jnp.exp(highest - peak[:, None])
        new_factor = jnp.exp(new_high - peak)
        all_totals = lax.optimization_barrier(jnp.sum(totals * cache_factor, axis=1)) + new_total * new_factor
        all_sums = lax.optimization_barrier(jnp.sum(sums * cache_factor[..., None], axis=1)) + new_sums * new_factor[..., None]
        return (all_sums / all_totals[..., None]).reshape(STEPS, HEADS * HEAD_DIM).astype(jnp.bfloat16)
    mixed = lax.map(one_row, jnp.arange(ROWS_ALL, dtype=jnp.int32))
    mixed = jnp.transpose(mixed, (1, 0, 2)).reshape(STEPS * ROWS_ALL, HEADS * HEAD_DIM)
    attended = jnp.dot(mixed, output_weight, preferred_element_type=jnp.float32)
    return attended.reshape(STEPS, ROWS_ALL, D).astype(jnp.bfloat16)
```

```python
import functools
import math

import jax
import jax.numpy as jnp
import numpy as np
from jax import lax
from jax.experimental import pallas as pl
from jax.experimental.pallas import tpu as pltpu
from jax.sharding import PartitionSpec as P

MESH = pl.DeviceIdType.MESH
F32 = jnp.float32
BF16 = jnp.bfloat16

ROWS = 8
STEPS = 2
KV_HEADS = 4
HEAD_DIM = 128
LOCAL_HEADS = 2
Q = LOCAL_HEADS * STEPS
RQ = ROWS * Q
SR = STEPS * ROWS
EPS = 1e-6
THETA = 1000000.0
FLOOR = -1e30
LOW = -1e29
QSCALE = HEAD_DIM**-0.5 * math.log2(math.e)


def iota(shape, dim):
    return lax.broadcasted_iota(jnp.int32, shape, dim)


def normed(x, gain):
    return x * lax.rsqrt(jnp.mean(x * x, axis=-1, keepdims=True) + EPS) * gain


def rotated(x, cos, sin):
    return x * cos + pltpu.roll(x, HEAD_DIM // 2, 1) * sin


def kernel(
    G, C, D, BLK,
    hidden_h, cache_h, lengths_h, source_h, target_h, wq_h, wkv_h, qgain_h, kgain_h, wo_h, freq_h,
    out_ref,
    hidden, cache, wq, wkv, wo, qgain, kgain, freq, lengths, source, target,
    z_send, z_recv, q_all, kv_send, kv_recv, q_rows, a_send, a_recv, mix, o_send, o_recv, y_send, y_recv,
    load_sem, cache_sem, zs_sem, zr_sem, qs_sem, qr_sem, ks_sem, kr_sem, as_sem, ar_sem, os_sem, or_sem, ys_sem, yr_sem,
):
    JJ = C // KV_HEADS
    KVW = 2 * KV_HEADS * HEAD_DIM // C
    PIECES = HEAD_DIM // KVW
    my_g = lax.axis_index("group")
    my_c = lax.axis_index("ctx")
    my_x = my_c // JJ
    my_low = lax.rem(my_c, JJ)

    loads = [
        (hidden_h, hidden), (wkv_h, wkv), (wq_h, wq), (lengths_h, lengths), (source_h, source), (target_h, target),
        (freq_h, freq), (qgain_h, qgain), (kgain_h, kgain), (wo_h, wo),
    ]
    loads = [pltpu.make_async_copy(a, b, load_sem.at[n]) for n, (a, b) in enumerate(loads)]
    for load in loads[:-1]:
        load.start()
    cache_loads = [pltpu.make_async_copy(cache_h.at[r], cache.at[r], cache_sem.at[r]) for r in range(ROWS)]
    for load in cache_loads:
        load.start()
    loads[-1].start()

    barrier = pltpu.get_barrier_semaphore()

    def greet(n, carry):
        pl.semaphore_signal(
            barrier, inc=1, device_id={"ctx": lax.rem(my_c + n, C)}, device_id_type=MESH
        )
        return carry

    for n in range(1, G):
        pl.semaphore_signal(barrier, inc=1, device_id={"group": lax.rem(my_g + n, G)}, device_id_type=MESH)
    lax.fori_loop(1, C, greet, 0)

    for load in loads[3:9]:
        load.wait()
    row_id = iota((SR, HEAD_DIM), 0)
    lane_id = iota((SR, HEAD_DIM), 1)
    slot_id = lax.rem(row_id, ROWS)
    position = row_id // ROWS
    for r in range(ROWS):
        position = position + jnp.where(slot_id == r, lengths[my_g * ROWS + r], 0)
    angle = position.astype(F32) * freq[...]
    cos = jnp.cos(angle)
    sin = jnp.sin(angle)
    sin = jnp.where(lane_id < HEAD_DIM // 2, -sin, sin)
    q_gain = qgain[...].astype(F32).reshape(1, HEAD_DIM) * QSCALE
    k_gain = kgain[...].astype(F32).reshape(1, HEAD_DIM)

    entries = source.shape[0]

    def slots(peer):
        away = jnp.int32(0)
        home = jnp.int32(0)
        for e in range(entries):
            s, t = source[e], target[e]
            away = away + jnp.where((s // ROWS == my_g) & (t // ROWS == peer), lax.rem(s, ROWS), 0)
            home = home + jnp.where((s // ROWS == peer) & (t // ROWS == my_g), lax.rem(t, ROWS), 0)
        return away, home

    ahead = [slots(lax.rem(my_g + n, G)) for n in range(1, G)]
    behind = [slots(lax.rem(my_g + G - n, G)) for n in range(1, G)]

    for load in loads[:3]:
        load.wait()
    h = jnp.concatenate([hidden[0], hidden[1]], axis=0)
    kv = jnp.dot(h, wkv[...], preferred_element_type=F32).astype(BF16).astype(F32)
    kv = jnp.concatenate([kv] * PIECES, axis=1)
    q = jnp.dot(h, wq[...], preferred_element_type=F32).astype(BF16).astype(F32)
    heads = [q[:, j * HEAD_DIM : (j + 1) * HEAD_DIM] for j in range(LOCAL_HEADS)] + [kv]

    for n in range(G - 1):
        message = jnp.zeros((SR, HEAD_DIM), F32)
        for j, x in enumerate(heads):
            picked = jnp.where(slot_id == ahead[n][1], x, 0.0)
            for s in range(STEPS):
                line = jnp.sum(picked[s * ROWS : (s + 1) * ROWS], axis=0, keepdims=True)
                message = jnp.where(row_id == j * STEPS + s, line, message)
        z_send[n] = message.astype(BF16)

    pl.semaphore_wait(barrier, C - 1 + G - 1)

    z_copies = [
        pltpu.make_async_remote_copy(
            src_ref=z_send.at[n], dst_ref=z_recv.at[n], send_sem=zs_sem.at[n], recv_sem=zr_sem.at[n],
            device_id={"group": lax.rem(my_g + n + 1, G)}, device_id_type=MESH,
        )
        for n in range(G - 1)
    ]
    for copy in z_copies:
        copy.start()
    for copy in z_copies:
        copy.wait_recv()
    for n in range(G - 1):
        came = z_recv[n].astype(F32)
        for j in range(len(heads)):
            for s in range(STEPS):
                line = came[j * STEPS + s : j * STEPS + s + 1, :]
                heads[j] = jnp.where((slot_id == behind[n][0]) & (row_id // ROWS == s), line, heads[j])

    for j in range(LOCAL_HEADS):
        turned = rotated(normed(heads[j], q_gain), cos, sin)
        for s in range(STEPS):
            q_rows[pl.ds(j * STEPS + s, ROWS, stride=Q), :] = turned[s * ROWS : (s + 1) * ROWS]
    q_mine = q_rows[...].astype(BF16)
    q_all[my_c] = q_mine
    kv_send[...] = heads[LOCAL_HEADS].astype(BF16)

    def q_copy(dest):
        return pltpu.make_async_remote_copy(
            src_ref=q_all.at[my_c], dst_ref=q_all.at[my_c], send_sem=qs_sem, recv_sem=qr_sem.at[my_x],
            device_id={"ctx": dest}, device_id_type=MESH,
        )

    def send_q(n, carry):
        q_copy(lax.rem(my_x + KV_HEADS - n // JJ, KV_HEADS) * JJ + lax.rem(my_low + n, JJ)).start()
        return carry

    lax.fori_loop(1, C, send_q, 0)

    kv_head = lax.rem(my_c, C // 2) // PIECES
    kv_slot = my_c // (C // 2) * PIECES + lax.rem(my_c, PIECES)

    def kv_copy(dest):
        return pltpu.make_async_remote_copy(
            src_ref=kv_send, dst_ref=kv_recv.at[kv_slot], send_sem=ks_sem, recv_sem=kr_sem.at[kv_slot],
            device_id={"ctx": dest}, device_id_type=MESH,
        )

    def send_kv(n, carry):
        dest = kv_head * JJ + n

        @pl.when(dest != my_c)
        def _():
            kv_copy(dest).start()

        return carry

    lax.fori_loop(0, JJ, send_kv, 0)

    @pl.when(kv_head == my_x)
    def _():
        kv_recv[kv_slot] = kv_send[...]

    ALL = JJ * RQ
    pi, pj = iota((ALL, ALL), 0), iota((ALL, ALL), 1)
    to_rows = pj == lax.rem(pi // Q, JJ) * RQ + pi // (JJ * Q) * Q + lax.rem(pi, Q)
    to_devices = pj == lax.rem(pi // Q, ROWS) * (JJ * Q) + pi // RQ * Q + lax.rem(pi, Q)
    to_rows = to_rows.astype(F32).astype(BF16)
    to_devices = to_devices.astype(F32).astype(BF16)
    gi, gj = iota((JJ * 16, 2 * ALL), 0), iota((JJ * 16, 2 * ALL), 1)
    gather = (
        (lax.rem(gi // 8, 2) == gj // ALL)
        & (gi // 16 == lax.rem(gj // Q, JJ))
        & (lax.rem(gi, Q) == lax.rem(gj, Q))
        & (lax.rem(gi // Q, 2) == lax.rem(gj // (JJ * Q), 2))
    ).astype(F32).astype(BF16)

    place = iota((JJ * Q, BLK), 1) + my_c * BLK
    lanes = iota((JJ * Q, HEAD_DIM), 1)
    for load in cache_loads:
        load.wait()

    def a_copy(dest):
        return pltpu.make_async_remote_copy(
            src_ref=a_send.at[dest], dst_ref=a_recv.at[my_c], send_sem=as_sem, recv_sem=ar_sem,
            device_id={"ctx": dest}, device_id_type=MESH,
        )

    def one_head(i, carry):
        g = lax.rem(my_x + i, KV_HEADS)

        @pl.when(i == 0)
        def _():
            if JJ > 1:
                some = q_all.at[pl.ds(0, JJ - 1)]
                pltpu.make_async_copy(some, some, qr_sem.at[g]).wait()

        @pl.when(i > 0)
        def _():
            some = q_all.at[pl.ds(0, JJ)]
            pltpu.make_async_copy(some, some, qr_sem.at[g]).wait()

        came = q_all[pl.ds(g * JJ, JJ)].reshape(ALL, HEAD_DIM)
        queries = jnp.dot(to_rows, came, preferred_element_type=F32).astype(BF16)
        k_at = pl.ds(pl.multiple_of(g * HEAD_DIM, HEAD_DIM), HEAD_DIM)
        v_at = pl.ds(pl.multiple_of((g + KV_HEADS) * HEAD_DIM, HEAD_DIM), HEAD_DIM)
        sums, peaks, totals = [], [], []
        for r in range(ROWS):
            scores = lax.dot_general(
                queries[r * JJ * Q : (r + 1) * JJ * Q], cache[r, :, k_at], (((1,), (1,)), ((), ())),
                preferred_element_type=F32,
            )
            scores = jnp.where(place < lengths[my_g * ROWS + r], scores, FLOOR)
            peak = jnp.maximum(jnp.max(scores, axis=1, keepdims=True), LOW).astype(BF16).astype(F32)
            weights = jnp.exp2(scores - peak)
            total = jnp.sum(weights, axis=1, keepdims=True)
            a = jnp.dot(weights.astype(BF16), cache[r, :, v_at], preferred_element_type=F32)
            high = total.astype(BF16).astype(F32)
            sums.append(a.astype(BF16))
            peaks.append(jnp.where(lanes & 3 == r // 2, peak, 0.0).astype(BF16))
            totals.append(
                jnp.where(lanes == r // 2, high, jnp.where(lanes == 4 + r // 2, total - high, 0.0)).astype(BF16)
            )
        sums = jnp.dot(to_devices, jnp.concatenate(sums, axis=0), preferred_element_type=F32)
        stats = jnp.dot(gather, jnp.concatenate(peaks + totals, axis=0), preferred_element_type=F32)
        a_send[pl.ds(g * JJ, JJ), :RQ] = sums.astype(BF16).reshape(JJ, RQ, HEAD_DIM)
        a_send[pl.ds(g * JJ, JJ), RQ:] = stats.astype(BF16).reshape(JJ, 16, HEAD_DIM)

        def send_a(n, carry):
            a_copy(g * JJ + lax.rem(my_low + n, JJ)).start()
            return carry

        lax.fori_loop(jnp.where(i == 0, 1, 0), JJ, send_a, 0)
        return carry

    lax.fori_loop(0, KV_HEADS, one_head, 0)
    a_recv[my_c] = a_send[my_c]

    def get_kv(n, carry):
        @pl.when(n // PIECES * (C // 2) + my_x * PIECES + lax.rem(n, PIECES) != my_c)
        def _():
            pltpu.make_async_copy(kv_send, kv_recv.at[n], kr_sem.at[n]).wait()

        return carry

    lax.fori_loop(0, 2 * PIECES, get_kv, 0)
    new = []
    for kind in range(2):
        x = kv_recv[kind * PIECES].astype(F32)
        for n in range(1, PIECES):
            x = jnp.where(lane_id // KVW == n, kv_recv[kind * PIECES + n].astype(F32), x)
        new.append(x)
    new_key = rotated(normed(new[0], k_gain), cos, sin).astype(BF16)
    new_value = new[1].astype(BF16)
    scores = lax.dot_general(q_mine, new_key, (((1,), (1,)), ((), ())), preferred_element_type=F32)
    ti, tj = iota((RQ, SR), 0), iota((RQ, SR), 1)
    scores = jnp.where((ti // Q == lax.rem(tj, ROWS)) & (tj // ROWS <= lax.rem(ti, STEPS)), scores, FLOOR)
    peak = jnp.max(scores, axis=1, keepdims=True)
    weights = jnp.exp2(scores - peak)
    total = jnp.sum(weights, axis=1, keepdims=True)
    new_sums = jnp.dot(weights.astype(BF16), new_value, preferred_element_type=F32)
    ui, uj = iota((RQ, HEAD_DIM), 0), iota((RQ, HEAD_DIM), 1)
    peak = jnp.where(uj & 3 == ui // 8, peak, 0.0)
    total = jnp.where(uj == ui // 8, total, 0.0)
    peak = peak[0:8] + peak[8:16] + peak[16:24] + peak[24:32]
    total = total[0:8] + total[8:16] + total[16:24] + total[24:32]

    some = a_recv.at[pl.ds(0, C - 1)]
    pltpu.make_async_copy(some, some, ar_sem).wait()
    stats = a_recv[:, RQ:].astype(F32)
    peaks = stats[:, :8]
    highest = jnp.maximum(jnp.max(peaks, axis=0), peak)
    scale = jnp.exp2(peaks - highest[None])
    new_scale = jnp.exp2(peak - highest)
    norm = jnp.sum(scale * stats[:, 8:], axis=0) + new_scale * total
    arrived = a_recv[:, :RQ].astype(F32)
    for k in range(RQ // 8):
        rows = slice(k * 8, (k + 1) * 8)
        acc = jnp.sum(arrived[:, rows] * scale[:, :, k : k + 1], axis=0) + new_sums[rows] * new_scale[:, k : k + 1]
        mix[rows, :] = acc / (norm[:, k : k + 1] + norm[:, 4 + k : 5 + k])
    mixed = jnp.concatenate(
        [
            jnp.concatenate([mix[pl.ds(j * STEPS + s, ROWS, stride=Q), :] for s in range(STEPS)], axis=0)
            for j in range(LOCAL_HEADS)
        ],
        axis=1,
    ).astype(BF16)

    loads[-1].wait()
    quarter = D // KV_HEADS
    width = D // C

    def o_copy(dest):
        return pltpu.make_async_remote_copy(
            src_ref=o_send.at[dest], dst_ref=o_recv.at[my_c], send_sem=os_sem, recv_sem=or_sem,
            device_id={"ctx": dest}, device_id_type=MESH,
        )

    def one_quarter(i, carry):
        g = lax.rem(my_x + i, KV_HEADS)
        part = jnp.dot(
            mixed, wo[:, pl.ds(pl.multiple_of(g * quarter, quarter), quarter)], preferred_element_type=F32
        ).astype(BF16)
        for n in range(JJ):
            o_send[g * JJ + n] = part[:, n * width : (n + 1) * width]

        def send_o(n, carry):
            o_copy(g * JJ + lax.rem(my_low + n, JJ)).start()
            return carry

        lax.fori_loop(jnp.where(i == 0, 1, 0), JJ, send_o, 0)
        return carry

    lax.fori_loop(0, KV_HEADS, one_quarter, 0)
    o_recv[my_c] = o_send[my_c]
    some = o_recv.at[pl.ds(0, C - 1)]
    pltpu.make_async_copy(some, some, or_sem).wait()
    result = jnp.sum(o_recv[...].astype(F32), axis=0)

    y_row = iota((8, HEAD_DIM), 0)
    for n in range(G - 1):
        picked = jnp.where(slot_id == ahead[n][0], result, 0.0)
        message = jnp.zeros((8, HEAD_DIM), F32)
        for s in range(STEPS):
            line = jnp.sum(picked[s * ROWS : (s + 1) * ROWS], axis=0, keepdims=True)
            message = jnp.where(y_row == s, line, message)
        y_send[n] = message
    y_copies = [
        pltpu.make_async_remote_copy(
            src_ref=y_send.at[n], dst_ref=y_recv.at[n], send_sem=ys_sem.at[n], recv_sem=yr_sem.at[n],
            device_id={"group": lax.rem(my_g + n + 1, G)}, device_id_type=MESH,
        )
        for n in range(G - 1)
    ]
    for copy in y_copies:
        copy.start()

    for copy in z_copies:
        copy.wait_send()
    some = q_all.at[pl.ds(0, C - 1)]
    pltpu.make_async_copy(some, some, qs_sem).wait()
    some = a_send.at[pl.ds(0, C - 1)]
    pltpu.make_async_copy(some, some, as_sem).wait()
    some = o_send.at[pl.ds(0, C - 1)]
    pltpu.make_async_copy(some, some, os_sem).wait()

    @pl.when(kv_head == my_x)
    def _():
        if JJ > 1:
            some = kv_recv.at[pl.ds(0, JJ - 1)]
            pltpu.make_async_copy(some, some, ks_sem).wait()

    @pl.when(kv_head != my_x)
    def _():
        some = kv_recv.at[pl.ds(0, JJ)]
        pltpu.make_async_copy(some, some, ks_sem).wait()

    for n, copy in enumerate(y_copies):
        copy.wait_recv()
        came = y_recv[n]
        for s in range(STEPS):
            result = jnp.where((slot_id == behind[n][1]) & (row_id // ROWS == s), came[s : s + 1], result)
    for copy in y_copies:
        copy.wait_send()
    out_ref[0] = result[:ROWS].astype(BF16)
    out_ref[1] = result[ROWS:].astype(BF16)


def per_device(G, C, hidden, cache, lengths, source, target, wq, wkv, qgain, kgain, wo):
    D = hidden.shape[-1]
    BLK = cache.shape[1]
    JJ = C // KV_HEADS
    pieces = C // 8
    half = np.arange(HEAD_DIM // 2, dtype=np.float64)
    freq = (THETA ** (-2.0 * half / HEAD_DIM)).astype(np.float32)
    freq = jnp.asarray(np.concatenate([freq, freq])[None])
    vmem = lambda x: pltpu.VMEM(x.shape, x.dtype)
    smem = lambda x: pltpu.SMEM(x.shape, x.dtype)
    dma = pltpu.SemaphoreType.DMA
    operands = (hidden, cache, lengths, source, target, wq, wkv, qgain, kgain, wo, freq)
    return pl.pallas_call(
        functools.partial(kernel, G, C, D, BLK),
        out_shape=jax.ShapeDtypeStruct((STEPS, ROWS, D // C), BF16),
        in_specs=[pl.BlockSpec(memory_space=pltpu.HBM)] * len(operands),
        out_specs=pl.BlockSpec(memory_space=pltpu.VMEM),
        scratch_shapes=[
            vmem(hidden), vmem(cache), vmem(wq), vmem(wkv), vmem(wo), vmem(qgain), vmem(kgain), vmem(freq),
            smem(lengths), smem(source), smem(target),
            pltpu.VMEM((G - 1, SR, HEAD_DIM), BF16),
            pltpu.VMEM((G - 1, SR, HEAD_DIM), BF16),
            pltpu.VMEM((C, RQ, HEAD_DIM), BF16),
            pltpu.VMEM((SR, HEAD_DIM), BF16),
            pltpu.VMEM((max(2 * pieces, JJ), SR, HEAD_DIM), BF16),
            pltpu.VMEM((RQ, HEAD_DIM), F32),
            pltpu.VMEM((C, RQ + 16, HEAD_DIM), BF16),
            pltpu.VMEM((C, RQ + 16, HEAD_DIM), BF16),
            pltpu.VMEM((RQ, HEAD_DIM), F32),
            pltpu.VMEM((C, SR, D // C), BF16),
            pltpu.VMEM((C, SR, D // C), BF16),
            pltpu.VMEM((G - 1, 8, HEAD_DIM), F32),
            pltpu.VMEM((G - 1, 8, HEAD_DIM), F32),
            dma((10,)), dma((ROWS,)), dma((G - 1,)), dma((G - 1,)), dma, dma((KV_HEADS,)), dma, dma((2 * pieces,)),
            dma, dma, dma, dma, dma((G - 1,)), dma((G - 1,)),
        ],
        compiler_params=pltpu.CompilerParams(
            collective_id=0, has_side_effects=True, vmem_limit_bytes=48 * 1024 * 1024
        ),
    )(*operands)


def solution(mesh):
    in_specs = (
        P(None, "group", None),
        P("group", "ctx", None),
        P(),
        P(),
        P(),
        P(None, "ctx"),
        P(None, "ctx"),
        P(),
        P(),
        P("ctx", None),
    )
    return jax.shard_map(
        functools.partial(per_device, mesh.shape["group"], mesh.shape["ctx"]),
        mesh=mesh, in_specs=in_specs, out_specs=P(None, "group", "ctx"), check_vma=False,
    )
```

```python
import functools
import math

import jax
import jax.numpy as jnp
import numpy as np
from jax import lax
from jax.experimental import pallas as pl
from jax.experimental.pallas import tpu as pltpu
from jax.sharding import PartitionSpec as P

MESH = pl.DeviceIdType.MESH
F32 = jnp.float32
BF16 = jnp.bfloat16

ROWS = 8
STEPS = 2
KV_HEADS = 4
HEAD_DIM = 128
LOCAL_HEADS = 2
Q = LOCAL_HEADS * STEPS
RQ = ROWS * Q
SR = STEPS * ROWS
HALF = RQ // 2
EPS = 1e-6
THETA = 1000000.0
FLOOR = -1e30
LOW = -1e29
PLANES = (1, 3, 2, 0)
FAR_FIRST = (2, 1, 3, 0)
QSCALE = HEAD_DIM**-0.5 * math.log2(math.e)


def iota(shape, dim):
    return lax.broadcasted_iota(jnp.int32, shape, dim)


def pick(order, n):
    return (sum(v << 2 * k for k, v in enumerate(order)) >> (2 * n)) & 3


def normed(x, gain):
    return x * lax.rsqrt(jnp.mean(x * x, axis=-1, keepdims=True) + EPS) * gain


def rotated(x, cos, sin):
    return x * cos + pltpu.roll(x, HEAD_DIM // 2, 1) * sin


def kernel(
    G, C, D, BLK,
    hidden_h, cache_h, lengths_h, source_h, target_h, wq_h, wkv_h, qgain_h, kgain_h, wo_h, freq_h,
    out_ref,
    hidden, cache, wq, wkv, wo, qgain, kgain, freq, lengths, source, target,
    raw, z_send, z_recv, pre, q_all, kv_pre, kv_send, kv_recv, a_send, a_recv, ml_send, ml_recv, mix,
    o_send, o_recv, y_send, y_recv,
    load_sem, cache_sem, zs_sem, zr_sem, qs_sem, qr_sem, ks_sem, kr_sem, as_sem, ar_sem, ms_sem, mr_sem,
    os_sem, or_sem, ys_sem, yr_sem,
):
    JJ = C // KV_HEADS
    J_BITS = JJ.bit_length() - 1
    KVW = 2 * KV_HEADS * HEAD_DIM // C
    PIECES = HEAD_DIM // KVW
    STAY = ROWS - (G - 1)
    my_g = lax.axis_index("group")
    my_c = lax.axis_index("ctx")
    my_x = my_c >> J_BITS
    my_low = my_c & (JJ - 1)
    drains = []

    def neighbour(plane, n):
        y = ((my_low >> 1) + pick(FAR_FIRST, n >> 1)) & (JJ // 2 - 1)
        return plane * JJ + y * 2 + ((my_low & 1) ^ (1 - (n & 1)))

    def remote(src, dst, send_sem, recv_sem, **dest):
        return pltpu.make_async_remote_copy(
            src_ref=src, dst_ref=dst, send_sem=send_sem, recv_sem=recv_sem, device_id=dest, device_id_type=MESH
        )

    def bytes_of(ref, sem):
        pltpu.make_async_copy(ref, ref, sem).wait()

    loads = [
        (hidden_h, hidden), (wkv_h, wkv), (wq_h, wq), (lengths_h, lengths), (source_h, source), (target_h, target),
        (freq_h, freq), (qgain_h, qgain), (kgain_h, kgain), (wo_h, wo),
    ]
    loads = [pltpu.make_async_copy(a, b, load_sem.at[n]) for n, (a, b) in enumerate(loads)]
    for load in loads[:-1]:
        load.start()
    cache_loads = [pltpu.make_async_copy(cache_h.at[r], cache.at[r], cache_sem.at[r]) for r in range(ROWS)]

    barrier = pltpu.get_barrier_semaphore()

    def greet(n, carry):
        pl.semaphore_signal(barrier, inc=1, device_id={"ctx": (my_c + n) & (C - 1)}, device_id_type=MESH)
        return carry

    for n in range(1, G):
        pl.semaphore_signal(barrier, inc=1, device_id={"group": (my_g + n) & (G - 1)}, device_id_type=MESH)
    lax.fori_loop(1, C, greet, 0)

    for load in loads[3:9]:
        load.wait()
    order = [jnp.int32(0)] * ROWS
    home = [jnp.int32(0)] * G
    listed = [False] * ROWS
    for e in range(source.shape[0]):
        s, t = source[e], target[e]
        off = ((t >> 3) - (s >> 3)) & (G - 1)
        out, back = (s >> 3) == my_g, (t >> 3) == my_g
        for n in range(1, G):
            order[STAY + n - 1] = order[STAY + n - 1] + jnp.where(out & (off == n), s & (ROWS - 1), 0)
            home[n] = home[n] + jnp.where(back & (off == G - n), t & (ROWS - 1), 0)
        for r in range(ROWS):
            listed[r] = listed[r] | (s == my_g * ROWS + r)
    count = jnp.int32(0)
    for r in range(ROWS):
        for n in range(min(r + 1, STAY)):
            order[n] = order[n] + jnp.where((count == n) & jnp.logical_not(listed[r]), r, 0)
        count = count + jnp.where(listed[r], 0, 1)
    row_lengths = [lengths[my_g * ROWS + order[r]] for r in range(ROWS)]

    table = (RQ + SR, HEAD_DIM)
    at, lane = iota(table, 0), iota(table, 1)
    row = jnp.where(at < RQ, at >> 2, (at - RQ) >> 1)
    position = at & 1
    for r in range(ROWS):
        position = position + jnp.where(row == r, row_lengths[r], 0)
    angle = position.astype(F32) * freq[...]
    cos = jnp.cos(angle)
    sin = jnp.sin(angle)
    sin = jnp.where(lane < HEAD_DIM // 2, -sin, sin)
    q_gain = qgain[...].astype(F32).reshape(1, HEAD_DIM) * QSCALE
    k_gain = kgain[...].astype(F32).reshape(1, HEAD_DIM)

    for load in loads[:3]:
        load.wait()
    for load in cache_loads:
        load.start()
    loads[-1].start()
    h = jnp.concatenate([hidden[0], hidden[1]], axis=0)
    q = jnp.dot(h, wq[...], preferred_element_type=F32).astype(BF16).astype(F32)
    kv = lax.dot_general(h, wkv[...], (((1,), (1,)), ((), ())), preferred_element_type=F32)
    kv = jnp.concatenate([kv.astype(BF16).astype(F32)] * PIECES, axis=1)
    parts = [q[:, j * HEAD_DIM : (j + 1) * HEAD_DIM] for j in range(LOCAL_HEADS)] + [kv]
    for n, x in enumerate(parts):
        for s in range(STEPS):
            raw[:, n * STEPS + s, :] = x[s * ROWS : (s + 1) * ROWS]
    raw[:, Q + STEPS :, :] = jnp.zeros((ROWS, 8 - Q - STEPS, HEAD_DIM), F32)
    for n in range(G - 1):
        z_send[n] = raw[home[n + 1]]

    def queries_of(half):
        rows = slice(half * HALF, (half + 1) * HALF)
        turned = rotated(normed(pre[rows, :], q_gain), cos[rows], sin[rows]).astype(BF16)
        q_all[half, my_c] = turned
        return turned

    for r in range(STAY):
        pre[r * Q : (r + 1) * Q, :] = raw[order[r], :Q, :]
        kv_pre[r * STEPS : (r + 1) * STEPS, :] = raw[order[r], Q : Q + STEPS, :]
    q_early = queries_of(0)
    pl.semaphore_wait(barrier, C - 1 + G - 1)

    z_copies = [
        remote(z_send.at[n], z_recv.at[n], zs_sem.at[n], zr_sem.at[n], group=(my_g + n + 1) & (G - 1))
        for n in range(G - 1)
    ]
    for copy in z_copies:
        copy.start()
    drains.append(lambda: [copy.wait_send() for copy in z_copies])

    def send_queries(half):
        def send_q(n, carry):
            plane = (my_x - pick(PLANES, n >> J_BITS)) & 3
            remote(
                q_all.at[half, my_c], q_all.at[half, my_c], qs_sem.at[half], qr_sem.at[half, my_x],
                ctx=neighbour(plane, n & (JJ - 1)),
            ).start()
            return carry

        lax.fori_loop(0, C - 1, send_q, 0)
        drains.append(lambda: bytes_of(q_all.at[half, pl.ds(0, C - 1)], qs_sem.at[half]))

    send_queries(0)

    ALL = JJ * HALF
    pi, pj = iota((ALL, ALL), 0), iota((ALL, ALL), 1)
    to_rows = pj == ((pi >> 2) & (JJ - 1)) * HALF + (pi >> (2 + J_BITS)) * Q + (pi & 3)
    to_devices = pj == ((pi >> 2) & 3) * (JJ * Q) + (pi >> 4) * Q + (pi & 3)
    to_rows = to_rows.astype(F32).astype(BF16)
    to_devices = to_devices.astype(F32).astype(BF16)
    gather = iota((JJ, 2 * ALL), 0) == ((iota((JJ, 2 * ALL), 1) >> 2) & (JJ - 1))
    gather = gather.astype(F32).astype(BF16)

    for copy in z_copies:
        copy.wait_recv()
    for n in range(1, G):
        r = STAY + n - 1
        pre[r * Q : (r + 1) * Q, :] = z_recv[G - 1 - n, :Q, :]
        kv_pre[r * STEPS : (r + 1) * STEPS, :] = z_recv[G - 1 - n, Q : Q + STEPS, :]
    q_late = queries_of(1)
    send_queries(1)

    kv_send[...] = kv_pre[...].astype(BF16)
    kv_bits = PIECES.bit_length() - 1
    kv_head = (my_c & (C // 2 - 1)) >> kv_bits
    kv_slot = ((my_c >> (C.bit_length() - 2)) << kv_bits) + (my_c & (PIECES - 1))

    def send_kv(n, carry):
        dest = kv_head * JJ + n

        @pl.when(dest != my_c)
        def _():
            remote(kv_send, kv_recv.at[kv_slot], ks_sem, kr_sem.at[kv_slot], ctx=dest).start()

        return carry

    lax.fori_loop(0, JJ, send_kv, 0)

    @pl.when(kv_head == my_x)
    def _():
        kv_recv[kv_slot] = kv_send[...]

    def drain_kv():
        @pl.when(kv_head == my_x)
        def _():
            if JJ > 1:
                bytes_of(kv_recv.at[pl.ds(0, JJ - 1)], ks_sem)

        @pl.when(kv_head != my_x)
        def _():
            bytes_of(kv_recv.at[pl.ds(0, JJ)], ks_sem)

    drains.append(drain_kv)

    place = iota((JJ * Q, BLK), 1) + my_c * BLK
    lanes = iota((JJ * Q, HEAD_DIM), 1) - (iota((JJ * Q, HEAD_DIM), 0) & 3)
    for load in cache_loads:
        load.wait()

    def attend(half):
        rows = range(half * ROWS // 2, (half + 1) * ROWS // 2)

        def one_plane(i, carry):
            g = (my_x + pick(PLANES, i)) & 3

            @pl.when(i == 3)
            def _():
                if JJ > 1:
                    bytes_of(q_all.at[half, pl.ds(0, JJ - 1)], qr_sem.at[half, g])

            @pl.when(i < 3)
            def _():
                bytes_of(q_all.at[half, pl.ds(0, JJ)], qr_sem.at[half, g])

            came = q_all[half, pl.ds(g * JJ, JJ)].reshape(ALL, HEAD_DIM)
            queries = jnp.dot(to_rows, came, preferred_element_type=F32).astype(BF16)
            k_at = pl.ds(pl.multiple_of(g * HEAD_DIM, HEAD_DIM), HEAD_DIM)
            v_at = pl.ds(pl.multiple_of((g + KV_HEADS) * HEAD_DIM, HEAD_DIM), HEAD_DIM)
            scores, peaks, weights, totals, sums, high, low = [], [], [], [], [], [], []
            for n, r in enumerate(rows):
                x = lax.dot_general(
                    queries[n * JJ * Q : (n + 1) * JJ * Q], cache[order[r], :, k_at], (((1,), (1,)), ((), ())),
                    preferred_element_type=F32,
                )
                scores.append(jnp.where(place < row_lengths[r], x, FLOOR))
            for x in scores:
                peaks.append(jnp.maximum(jnp.max(x, axis=1, keepdims=True), LOW).astype(BF16).astype(F32))
            for x, peak in zip(scores, peaks):
                x = jnp.exp2(x - peak)
                totals.append(jnp.sum(x, axis=1, keepdims=True))
                weights.append(x.astype(BF16))
            for x, r in zip(weights, rows):
                sums.append(jnp.dot(x, cache[order[r], :, v_at], preferred_element_type=F32).astype(BF16))
            for n, (peak, total) in enumerate(zip(peaks, totals)):
                rounded = total.astype(BF16).astype(F32)
                x = jnp.where(lanes == n * Q, peak, jnp.where(lanes == HALF + n * Q, rounded, 0.0))
                high.append(x.astype(BF16))
                low.append(jnp.where(lanes == HALF + n * Q, total - rounded, 0.0).astype(BF16))
            sums = jnp.dot(to_devices, jnp.concatenate(sums, axis=0), preferred_element_type=F32)
            stats = jnp.dot(gather, jnp.concatenate(high + low, axis=0), preferred_element_type=F32)
            a_send[half, pl.ds(g * JJ, JJ)] = sums.astype(BF16).reshape(JJ, HALF, HEAD_DIM)
            ml_send[half, pl.ds(g * JJ, JJ), 0, :] = stats

            def send_a(n, carry):
                dest = neighbour(g, n)
                remote(
                    a_send.at[half, dest], a_recv.at[half, my_c], as_sem.at[half], ar_sem.at[half], ctx=dest
                ).start()
                remote(
                    ml_send.at[half, dest], ml_recv.at[half, my_c], ms_sem.at[half], mr_sem.at[half], ctx=dest
                ).start()
                return carry

            lax.fori_loop(0, jnp.where(i == 3, JJ - 1, JJ), send_a, 0)
            return carry

        lax.fori_loop(0, KV_HEADS, one_plane, 0)
        drains.append(lambda: bytes_of(a_send.at[half, pl.ds(0, C - 1)], as_sem.at[half]))
        drains.append(lambda: bytes_of(ml_send.at[half, pl.ds(0, C - 1)], ms_sem.at[half]))
        a_recv[half, my_c] = a_send[half, my_c]
        ml_recv[half, my_c] = ml_send[half, my_c]

    attend(0)
    attend(1)

    def get_kv(n, carry):
        @pl.when((n >> kv_bits) * (C // 2) + my_x * PIECES + (n & (PIECES - 1)) != my_c)
        def _():
            bytes_of(kv_recv.at[n], kr_sem.at[n])

        return carry

    lax.fori_loop(0, 2 * PIECES, get_kv, 0)
    new = []
    piece = iota((SR, HEAD_DIM), 1) >> (KVW.bit_length() - 1)
    for kind in range(2):
        x = kv_recv[kind * PIECES].astype(F32)
        for n in range(1, PIECES):
            x = jnp.where(piece == n, kv_recv[kind * PIECES + n].astype(F32), x)
        new.append(x)
    new_key = rotated(normed(new[0], k_gain), cos[RQ:], sin[RQ:]).astype(BF16)
    new_value = new[1].astype(BF16)
    q_mine = jnp.concatenate([q_early, q_late], axis=0)
    scores = lax.dot_general(q_mine, new_key, (((1,), (1,)), ((), ())), preferred_element_type=F32)
    ti, tj = iota((RQ, SR), 0), iota((RQ, SR), 1)
    scores = jnp.where(((ti >> 2) == (tj >> 1)) & ((tj & 1) <= (ti & 1)), scores, FLOOR)
    new_peak = jnp.max(scores, axis=1, keepdims=True)
    weights = jnp.exp2(scores - new_peak)
    new_total = jnp.sum(weights, axis=1, keepdims=True)
    new_sums = jnp.dot(weights.astype(BF16), new_value, preferred_element_type=F32)

    for half in range(2):
        bytes_of(ml_recv.at[half, pl.ds(0, C - 1)], mr_sem.at[half])
        rows = slice(half * HALF, (half + 1) * HALF)
        stats = jnp.transpose(ml_recv[half, :, 0, :])
        peaks, totals = stats[:HALF], stats[HALF : 2 * HALF]
        highest = jnp.maximum(jnp.max(peaks, axis=1, keepdims=True), new_peak[rows])
        scale = jnp.exp2(peaks - highest)
        new_scale = jnp.exp2(new_peak[rows] - highest)
        norm = jnp.sum(scale * totals, axis=1, keepdims=True) + new_scale * new_total[rows]
        bytes_of(a_recv.at[half, pl.ds(0, C - 1)], ar_sem.at[half])
        acc = new_sums[rows] * new_scale
        for n in range(C):
            acc = acc + a_recv[half, n].astype(F32) * scale[:, n : n + 1]
        mix[rows, :] = acc / norm
    mixed = jnp.concatenate(
        [
            jnp.concatenate([mix[pl.ds(j * STEPS + s, ROWS, stride=Q), :] for s in range(STEPS)], axis=0)
            for j in range(LOCAL_HEADS)
        ],
        axis=1,
    ).astype(BF16)

    loads[-1].wait()
    quarter = D // KV_HEADS
    width = D // C

    def one_quarter(i, carry):
        g = (my_x + pick(FAR_FIRST, i)) & 3
        part = jnp.dot(
            mixed, wo[:, pl.ds(pl.multiple_of(g * quarter, quarter), quarter)], preferred_element_type=F32
        ).astype(BF16)
        for n in range(JJ):
            o_send[g * JJ + n] = part[:, n * width : (n + 1) * width]

        def send_o(n, carry):
            dest = neighbour(g, n)
            remote(o_send.at[dest], o_recv.at[my_c], os_sem, or_sem, ctx=dest).start()
            return carry

        lax.fori_loop(0, jnp.where(i == 3, JJ - 1, JJ), send_o, 0)
        return carry

    lax.fori_loop(0, KV_HEADS, one_quarter, 0)
    drains.append(lambda: bytes_of(o_send.at[pl.ds(0, C - 1)], os_sem))
    o_recv[my_c] = o_send[my_c]
    bytes_of(o_recv.at[pl.ds(0, C - 1)], or_sem)
    result = jnp.sum(o_recv[...].astype(F32), axis=0)

    for n in range(G - 1):
        for s in range(STEPS):
            y_send[n, s : s + 1, :] = result[s * ROWS + STAY + n : s * ROWS + STAY + n + 1]
        y_send[n, STEPS:, :] = jnp.zeros((8 - STEPS, HEAD_DIM), F32)
    y_copies = [
        remote(y_send.at[n], y_recv.at[n], ys_sem.at[n], yr_sem.at[n], group=(my_g + n + 1) & (G - 1))
        for n in range(G - 1)
    ]
    for copy in y_copies:
        copy.start()

    for drain in drains:
        drain()

    slot = iota((ROWS, HEAD_DIM), 0)
    lines = [jnp.zeros((ROWS, HEAD_DIM), F32)] * STEPS
    for s in range(STEPS):
        for r in range(STAY):
            lines[s] = jnp.where(slot == order[r], result[s * ROWS + r : s * ROWS + r + 1], lines[s])
    for n, copy in enumerate(y_copies):
        copy.wait_recv()
        for s in range(STEPS):
            lines[s] = jnp.where(slot == home[G - 1 - n], y_recv[n, s : s + 1, :], lines[s])
    for copy in y_copies:
        copy.wait_send()
    for s in range(STEPS):
        out_ref[s] = lines[s].astype(BF16)


def per_device(G, C, hidden, cache, lengths, source, target, wq, wkv, qgain, kgain, wo):
    D = hidden.shape[-1]
    BLK = cache.shape[1]
    JJ = C // KV_HEADS
    pieces = C // 8
    half = np.arange(HEAD_DIM // 2, dtype=np.float64)
    freq = (THETA ** (-2.0 * half / HEAD_DIM)).astype(np.float32)
    freq = jnp.asarray(np.concatenate([freq, freq])[None])
    vmem = lambda x: pltpu.VMEM(x.shape, x.dtype)
    smem = lambda x: pltpu.SMEM(x.shape, x.dtype)
    dma = pltpu.SemaphoreType.DMA
    wkv = wkv.T
    operands = (hidden, cache, lengths, source, target, wq, wkv, qgain, kgain, wo, freq)
    return pl.pallas_call(
        functools.partial(kernel, G, C, D, BLK),
        out_shape=jax.ShapeDtypeStruct((STEPS, ROWS, D // C), BF16),
        in_specs=[pl.BlockSpec(memory_space=pltpu.HBM)] * len(operands),
        out_specs=pl.BlockSpec(memory_space=pltpu.VMEM),
        scratch_shapes=[
            vmem(hidden), vmem(cache), vmem(wq), vmem(wkv), vmem(wo), vmem(qgain), vmem(kgain), vmem(freq),
            smem(lengths), smem(source), smem(target),
            pltpu.VMEM((ROWS, 8, HEAD_DIM), F32),
            pltpu.VMEM((G - 1, 8, HEAD_DIM), F32),
            pltpu.VMEM((G - 1, 8, HEAD_DIM), F32),
            pltpu.VMEM((RQ, HEAD_DIM), F32),
            pltpu.VMEM((2, C, HALF, HEAD_DIM), BF16),
            pltpu.VMEM((SR, HEAD_DIM), F32),
            pltpu.VMEM((SR, HEAD_DIM), BF16),
            pltpu.VMEM((max(2 * pieces, JJ), SR, HEAD_DIM), BF16),
            pltpu.VMEM((2, C, HALF, HEAD_DIM), BF16),
            pltpu.VMEM((2, C, HALF, HEAD_DIM), BF16),
            pltpu.VMEM((2, C, 1, HEAD_DIM), F32),
            pltpu.VMEM((2, C, 1, HEAD_DIM), F32),
            pltpu.VMEM((RQ, HEAD_DIM), F32),
            pltpu.VMEM((C, SR, D // C), BF16),
            pltpu.VMEM((C, SR, D // C), BF16),
            pltpu.VMEM((G - 1, 8, HEAD_DIM), F32),
            pltpu.VMEM((G - 1, 8, HEAD_DIM), F32),
            dma((10,)), dma((ROWS,)), dma((G - 1,)), dma((G - 1,)), dma((2,)), dma((2, KV_HEADS)), dma,
            dma((2 * pieces,)), dma((2,)), dma((2,)), dma((2,)), dma((2,)), dma, dma, dma((G - 1,)), dma((G - 1,)),
        ],
        compiler_params=pltpu.CompilerParams(
            collective_id=0, has_side_effects=True, vmem_limit_bytes=62 * 1024 * 1024
        ),
    )(*operands)


def solution(mesh):
    in_specs = (
        P(None, "group", None),
        P("group", "ctx", None),
        P(),
        P(),
        P(),
        P(None, "ctx"),
        P(None, "ctx"),
        P(),
        P(),
        P("ctx", None),
    )
    return jax.shard_map(
        functools.partial(per_device, mesh.shape["group"], mesh.shape["ctx"]),
        mesh=mesh, in_specs=in_specs, out_specs=P(None, "group", "ctx"), check_vma=False,
    )
```

```python
import functools
import math

import jax
import jax.numpy as jnp
import numpy as np
from jax import lax
from jax.experimental import pallas as pl
from jax.experimental.pallas import tpu as pltpu
from jax.sharding import PartitionSpec as P

MESH = pl.DeviceIdType.MESH
F32 = jnp.float32
BF16 = jnp.bfloat16

ROWS = 8
STEPS = 2
KV_HEADS = 4
HEAD_DIM = 128
LOCAL_HEADS = 2
Q = LOCAL_HEADS * STEPS
RQ = ROWS * Q
SR = STEPS * ROWS
CHUNKS = 4
HALF = RQ // 2
EPS = 1e-6
THETA = 1000000.0
FLOOR = -1e30
LOW = -1e29
FAR_FIRST = (2, 3, 1, 0)
QSCALE = HEAD_DIM**-0.5 * math.log2(math.e)


def iota(shape, dim):
    return lax.broadcasted_iota(jnp.int32, shape, dim)


def pick(order, n):
    if isinstance(n, int):
        return order[n]
    return (sum(v << 2 * k for k, v in enumerate(order)) >> (2 * n)) & 3


def normed(x, gain):
    return x * lax.rsqrt(jnp.mean(x * x, axis=-1, keepdims=True) + EPS) * gain


def rotated(x, cos, sin):
    return x * cos + pltpu.roll(x, HEAD_DIM // 2, 1) * sin


def kernel(
    G, C, D, BLK,
    hidden_h, cache_h, lengths_h, source_h, target_h, wq_h, wkv_h, qgain_h, kgain_h, wo_h, freq_h,
    out_ref,
    hidden, cache, wq, wkv, wo, qgain, kgain, freq, lengths, source, target,
    raw, z_send, z_recv, pre, q_early, q_late, kv_pre, kv_send, kv_recv, a_send_early, a_send_late,
    a_recv_early, a_recv_late, ml_send, ml_recv, mix,
    o_send, o_recv, y_send, y_recv,
    load_sem, cache_sem, zs_sem, zr_sem, qs_sem, qr_sem, ks_sem, kr_sem, as_sem, ar_sem, ms_sem, mr_sem,
    os_sem, or_sem, ys_sem, yr_sem,
):
    JJ = C // KV_HEADS
    J_BITS = JJ.bit_length() - 1
    KVW = 2 * KV_HEADS * HEAD_DIM // C
    PIECES = HEAD_DIM // KVW
    STAY = ROWS - (G - 1)
    my_g = lax.axis_index("group")
    my_c = lax.axis_index("ctx")
    my_x = my_c >> J_BITS
    my_low = my_c & (JJ - 1)
    drains = []
    q_all = (q_early, q_late)
    a_send, a_recv = (a_send_early, a_send_late), (a_recv_early, a_recv_late)
    halves = (range(ROWS // 2), range(ROWS // 2, ROWS))

    def neighbour(plane, n):
        y = ((my_low >> 1) ^ pick(FAR_FIRST, n >> 1)) & (JJ // 2 - 1)
        return plane * JJ + y * 2 + ((my_low & 1) ^ (1 - (n & 1)))

    def remote(src, dst, send_sem, recv_sem, **dest):
        return pltpu.make_async_remote_copy(
            src_ref=src, dst_ref=dst, send_sem=send_sem, recv_sem=recv_sem, device_id=dest, device_id_type=MESH
        )

    def bytes_of(ref, sem):
        pltpu.make_async_copy(ref, ref, sem).wait()

    barrier = pltpu.get_barrier_semaphore()
    for n in range(1, G):
        pl.semaphore_signal(barrier, inc=1, device_id={"group": (my_g + n) & (G - 1)}, device_id_type=MESH)

    def greet(n, carry):
        dest = neighbour(my_x ^ pick(FAR_FIRST, n >> J_BITS), n & (JJ - 1))
        pl.semaphore_signal(barrier, inc=1, device_id={"ctx": dest}, device_id_type=MESH)
        return carry

    lax.fori_loop(0, JJ, greet, 0)
    depth = D // CHUNKS
    copies = [(hidden_h, hidden), (wkv_h, wkv)]
    copies += [(wq_h.at[pl.ds(n * depth, depth)], wq.at[pl.ds(n * depth, depth)]) for n in range(CHUNKS)]
    copies += [(source_h, source), (target_h, target), (lengths_h, lengths), (freq_h, freq), (qgain_h, qgain)]
    copies += [(kgain_h, kgain), (wo_h, wo)]
    loads = [pltpu.make_async_copy(a, b, load_sem.at[n]) for n, (a, b) in enumerate(copies)]
    for load in loads[:-1]:
        load.start()
    cache_loads = [pltpu.make_async_copy(cache_h.at[r], cache.at[r], cache_sem.at[r]) for r in range(ROWS)]
    lax.fori_loop(JJ, C - 1, greet, 0)

    for load in loads[2 + CHUNKS : -1]:
        load.wait()
    order = [jnp.int32(0)] * ROWS
    home = [jnp.int32(0)] * G
    listed = [False] * ROWS
    for e in range(source.shape[0]):
        s, t = source[e], target[e]
        off = ((t >> 3) - (s >> 3)) & (G - 1)
        out, back = (s >> 3) == my_g, (t >> 3) == my_g
        for n in range(1, G):
            order[STAY + n - 1] = order[STAY + n - 1] + jnp.where(out & (off == n), s & (ROWS - 1), 0)
            home[n] = home[n] + jnp.where(back & (off == G - n), t & (ROWS - 1), 0)
        for r in range(ROWS):
            listed[r] = listed[r] | (s == my_g * ROWS + r)
    count = jnp.int32(0)
    for r in range(ROWS):
        for n in range(min(r + 1, STAY)):
            order[n] = order[n] + jnp.where((count == n) & jnp.logical_not(listed[r]), r, 0)
        count = count + jnp.where(listed[r], 0, 1)
    row_lengths = [lengths[my_g * ROWS + order[r]] for r in range(ROWS)]

    at, lane = iota((RQ + SR, HEAD_DIM), 0), iota((RQ + SR, HEAD_DIM), 1)
    row = jnp.where(at < RQ, at >> 2, (at - RQ) >> 1)
    position = at & 1
    for r in range(ROWS):
        position = position + jnp.where(row == r, row_lengths[r], 0)
    angle = position.astype(F32) * freq[...]
    cos = jnp.cos(angle)
    sin = jnp.sin(angle)
    sin = jnp.where(lane < HEAD_DIM // 2, -sin, sin)
    q_gain = qgain[...].astype(F32).reshape(1, HEAD_DIM) * QSCALE
    k_gain = kgain[...].astype(F32).reshape(1, HEAD_DIM)

    loads[0].wait()
    h = jnp.concatenate([hidden[0], hidden[1]], axis=0)
    loads[1].wait()
    kv = lax.dot_general(h, wkv[...], (((1,), (1,)), ((), ())), preferred_element_type=F32)
    kv = jnp.concatenate([kv.astype(BF16).astype(F32)] * PIECES, axis=1)
    q = jnp.zeros((SR, wq.shape[1]), F32)
    for n in range(CHUNKS):
        loads[2 + n].wait()
        if n == CHUNKS - 1:
            for load in cache_loads:
                load.start()
            loads[-1].start()
        at = slice(n * depth, (n + 1) * depth)
        q = q + jnp.dot(h[:, at], wq[at, :], preferred_element_type=F32)
    q = q.astype(BF16).astype(F32)
    parts = [q[:, j * HEAD_DIM : (j + 1) * HEAD_DIM] for j in range(LOCAL_HEADS)] + [kv]
    for n, x in enumerate(parts):
        for s in range(STEPS):
            raw[:, n * STEPS + s, :] = x[s * ROWS : (s + 1) * ROWS]
    raw[:, Q + STEPS :, :] = jnp.zeros((ROWS, 8 - Q - STEPS, HEAD_DIM), F32)
    for n in range(G - 1):
        z_send[n] = raw[home[n + 1]]

    pl.semaphore_wait(barrier, C - 1 + G - 1)

    z_copies = [
        remote(z_send.at[n], z_recv.at[n], zs_sem.at[n], zr_sem.at[n], group=(my_g + n + 1) & (G - 1))
        for n in range(G - 1)
    ]
    for copy in z_copies:
        copy.start()
    drains.append(lambda: [copy.wait_send() for copy in z_copies])

    def send_queries(half):
        rows = slice(half * HALF, (half + 1) * HALF)
        turned = rotated(normed(pre[rows, :], q_gain), cos[rows], sin[rows]).astype(BF16)
        q_all[half][my_c] = turned

        def send_q(n, carry):
            dest = neighbour(my_x ^ pick(FAR_FIRST, n >> J_BITS), n & (JJ - 1))
            remote(
                q_all[half].at[my_c], q_all[half].at[my_c], qs_sem.at[half], qr_sem.at[half, my_x], ctx=dest
            ).start()
            return carry

        lax.fori_loop(0, C - 1, send_q, 0)
        drains.append(lambda: bytes_of(q_all[half].at[pl.ds(0, C - 1)], qs_sem.at[half]))
        return turned

    for r in range(STAY):
        pre[r * Q : (r + 1) * Q, :] = raw[order[r], :Q, :]
        kv_pre[r * STEPS : (r + 1) * STEPS, :] = raw[order[r], Q : Q + STEPS, :]
    queries = [send_queries(0)]

    ALL = JJ * HALF
    at, to = iota((ALL, ALL), 0), iota((ALL, ALL), 1)
    to_rows = to == ((at >> 2) & (JJ - 1)) * HALF + (at >> (2 + J_BITS)) * Q + (at & 3)
    to_devices = to == ((at >> 2) & 3) * (JJ * Q) + (at >> 4) * Q + (at & 3)
    to_rows = to_rows.astype(F32).astype(BF16)
    to_devices = to_devices.astype(F32).astype(BF16)
    gather = iota((JJ, 2 * ALL), 0) == ((iota((JJ, 2 * ALL), 1) >> 2) & (JJ - 1))
    gather = gather.astype(F32).astype(BF16)

    for copy in z_copies:
        copy.wait_recv()
    for n in range(1, G):
        r = STAY + n - 1
        pre[r * Q : (r + 1) * Q, :] = z_recv[G - 1 - n, :Q, :]
        kv_pre[r * STEPS : (r + 1) * STEPS, :] = z_recv[G - 1 - n, Q : Q + STEPS, :]
    queries.append(send_queries(1))

    kv_send[...] = kv_pre[...].astype(BF16)
    kv_bits = PIECES.bit_length() - 1
    kv_head = (my_c & (C // 2 - 1)) >> kv_bits
    kv_slot = ((my_c >> (C.bit_length() - 2)) << kv_bits) + (my_c & (PIECES - 1))

    def send_kv(n, carry):
        dest = kv_head * JJ + n

        @pl.when(dest != my_c)
        def _():
            remote(kv_send, kv_recv.at[kv_slot], ks_sem, kr_sem.at[kv_slot], ctx=dest).start()

        return carry

    lax.fori_loop(0, JJ, send_kv, 0)

    @pl.when(kv_head == my_x)
    def _():
        kv_recv[kv_slot] = kv_send[...]

    def drain_kv():
        @pl.when(kv_head == my_x)
        def _():
            if JJ > 1:
                bytes_of(kv_recv.at[pl.ds(0, JJ - 1)], ks_sem)

        @pl.when(kv_head != my_x)
        def _():
            bytes_of(kv_recv.at[pl.ds(0, JJ)], ks_sem)

    drains.append(drain_kv)

    M = JJ * Q
    place = iota((2 * M, BLK), 1) + my_c * BLK
    lanes = iota((2 * M, HEAD_DIM), 1) - (iota((2 * M, HEAD_DIM), 0) & 3)
    for load in cache_loads:
        load.wait()

    def attend(half):
        rows = halves[half]
        send, recv = a_send[half], a_recv[half]

        for x in FAR_FIRST:
            if JJ > (x == 0):
                bytes_of(q_all[half].at[pl.ds(0, JJ - (x == 0))], qr_sem.at[half, my_x ^ x])

        def two_planes(i):
            first = (my_x & 2) ^ (2 - 2 * i)
            nearer = my_x ^ (3 - 2 * i)
            last = my_x ^ (2 - 2 * i)
            k_at = pl.ds(pl.multiple_of(first * HEAD_DIM, 2 * HEAD_DIM), 2 * HEAD_DIM)
            v_at = pl.ds(pl.multiple_of((first + KV_HEADS) * HEAD_DIM, 2 * HEAD_DIM), 2 * HEAD_DIM)
            came = [q_all[half][pl.ds((first + m) * JJ, JJ)].reshape(ALL, HEAD_DIM) for m in range(2)]
            came = [jnp.dot(to_rows, x, preferred_element_type=F32).astype(BF16) for x in came]
            blank = jnp.zeros((M, HEAD_DIM), BF16)
            scores, peaks, weights, totals, sums, high, low = [], [], [], [], [], [], []
            for n, r in enumerate(rows):
                a, b = [x[n * M : (n + 1) * M] for x in came]
                both = jnp.concatenate(
                    [jnp.concatenate([a, blank], axis=1), jnp.concatenate([blank, b], axis=1)], axis=0
                )
                x = lax.dot_general(
                    both, cache[order[r], :, k_at], (((1,), (1,)), ((), ())), preferred_element_type=F32
                )
                scores.append(jnp.where(place < row_lengths[r], x, FLOOR))
            for x in scores:
                peaks.append(jnp.maximum(jnp.max(x, axis=1, keepdims=True), LOW).astype(BF16).astype(F32))
            for x, peak in zip(scores, peaks):
                x = jnp.exp2(x - peak)
                totals.append(jnp.sum(x, axis=1, keepdims=True))
                weights.append(x.astype(BF16))
            for x, r in zip(weights, rows):
                sums.append(jnp.dot(x, cache[order[r], :, v_at], preferred_element_type=F32).astype(BF16))
            for n, (peak, total) in enumerate(zip(peaks, totals)):
                rounded = total.astype(BF16).astype(F32)
                n = rows[n] * Q
                x = jnp.where(lanes == n, peak, jnp.where(lanes == RQ + n, rounded, 0.0))
                high.append(x.astype(BF16))
                low.append(jnp.where(lanes == RQ + n, total - rounded, 0.0).astype(BF16))
            for m in range(2):
                mine = slice(m * M, (m + 1) * M)
                x = jnp.concatenate([x[mine, m * HEAD_DIM : (m + 1) * HEAD_DIM] for x in sums], axis=0)
                x = jnp.dot(to_devices, x, preferred_element_type=F32)
                send[pl.ds((first + m) * JJ, JJ)] = x.astype(BF16).reshape(JJ, HALF, HEAD_DIM)
                x = jnp.concatenate([x[mine] for x in high + low], axis=0)
                x = jnp.dot(gather, x, preferred_element_type=F32)
                if half:
                    x = x + ml_send[pl.ds((first + m) * JJ, JJ), 0, :]
                ml_send[pl.ds((first + m) * JJ, JJ), 0, :] = x

            def send_to(n, carry):
                dest = neighbour(jnp.where((n >= JJ) == (i == 1), last, nearer), n & (JJ - 1))
                remote(send.at[dest], recv.at[my_c], as_sem.at[half], ar_sem.at[half], ctx=dest).start()
                if half:
                    remote(ml_send.at[dest], ml_recv.at[my_c], ms_sem, mr_sem, ctx=dest).start()

                return carry

            lax.fori_loop(0, 2 * JJ - i, send_to, 0)

        two_planes(0)
        two_planes(1)
        drains.append(lambda: bytes_of(send.at[pl.ds(0, C - 1)], as_sem.at[half]))
        recv[my_c] = send[my_c]

    attend(0)
    attend(1)
    ml_recv[my_c] = ml_send[my_c]
    drains.append(lambda: bytes_of(ml_send.at[pl.ds(0, C - 1)], ms_sem))

    def get_kv(n, carry):
        @pl.when((n >> kv_bits) * (C // 2) + my_x * PIECES + (n & (PIECES - 1)) != my_c)
        def _():
            bytes_of(kv_recv.at[n], kr_sem.at[n])

        return carry

    lax.fori_loop(0, 2 * PIECES, get_kv, 0)
    new = []
    piece = iota((SR, HEAD_DIM), 1) >> (KVW.bit_length() - 1)
    for kind in range(2):
        x = kv_recv[kind * PIECES].astype(F32)
        for n in range(1, PIECES):
            x = jnp.where(piece == n, kv_recv[kind * PIECES + n].astype(F32), x)
        new.append(x)
    new_key = rotated(normed(new[0], k_gain), cos[RQ:], sin[RQ:]).astype(BF16)
    new_value = new[1].astype(BF16)
    q_mine = jnp.concatenate(queries, axis=0)
    scores = lax.dot_general(q_mine, new_key, (((1,), (1,)), ((), ())), preferred_element_type=F32)
    ti, tj = iota(scores.shape, 0), iota(scores.shape, 1)
    scores = jnp.where(((ti >> 2) == (tj >> 1)) & ((tj & 1) <= (ti & 1)), scores, FLOOR)
    new_peak = jnp.max(scores, axis=1, keepdims=True)
    weights = jnp.exp2(scores - new_peak)
    new_total = jnp.sum(weights, axis=1, keepdims=True)
    new_sums = jnp.dot(weights.astype(BF16), new_value, preferred_element_type=F32)

    bytes_of(ml_recv.at[pl.ds(0, C - 1)], mr_sem)
    stats = jnp.transpose(ml_recv[:, 0, :])
    peaks, totals = stats[:RQ], stats[RQ : 2 * RQ]
    highest = jnp.maximum(jnp.max(peaks, axis=1, keepdims=True), new_peak)
    scale = jnp.exp2(peaks - highest)
    new_scale = jnp.exp2(new_peak - highest)
    norm = jnp.sum(scale * totals, axis=1, keepdims=True) + new_scale * new_total
    for half in range(2):
        bytes_of(a_recv[half].at[pl.ds(0, C - 1)], ar_sem.at[half])
        rows = slice(half * HALF, (half + 1) * HALF)
        acc = [(new_sums * new_scale)[rows]] + [jnp.zeros((HALF, HEAD_DIM), F32)] * 3
        for n in range(C):
            acc[n & 3] = acc[n & 3] + a_recv[half][n].astype(F32) * scale[rows, n : n + 1]
        mix[rows, :] = ((acc[0] + acc[1]) + (acc[2] + acc[3])) / norm[rows]
    mixed = jnp.concatenate(
        [
            jnp.concatenate([mix[pl.ds(j * STEPS + s, ROWS, stride=Q), :] for s in range(STEPS)], axis=0)
            for j in range(LOCAL_HEADS)
        ],
        axis=1,
    ).astype(BF16)

    loads[-1].wait()
    quarter = D // KV_HEADS
    width = D // C

    for i in range(KV_HEADS):
        g = my_x ^ FAR_FIRST[i]
        part = jnp.dot(
            mixed, wo[:, pl.ds(pl.multiple_of(g * quarter, quarter), quarter)], preferred_element_type=F32
        ).astype(BF16)
        for n in range(JJ):
            o_send[g * JJ + n] = part[:, n * width : (n + 1) * width]

        def send_o(n, carry):
            dest = neighbour(g, n)
            remote(o_send.at[dest], o_recv.at[my_c], os_sem, or_sem, ctx=dest).start()
            return carry

        lax.fori_loop(0, JJ - (FAR_FIRST[i] == 0), send_o, 0)
    drains.append(lambda: bytes_of(o_send.at[pl.ds(0, C - 1)], os_sem))
    o_recv[my_c] = o_send[my_c]
    bytes_of(o_recv.at[pl.ds(0, C - 1)], or_sem)
    result = jnp.sum(o_recv[...].astype(F32), axis=0)

    for n in range(G - 1):
        for s in range(STEPS):
            y_send[n, s : s + 1, :] = result[s * ROWS + STAY + n : s * ROWS + STAY + n + 1]
        y_send[n, STEPS:, :] = jnp.zeros((8 - STEPS, HEAD_DIM), F32)
    y_copies = [
        remote(y_send.at[n], y_recv.at[n], ys_sem.at[n], yr_sem.at[n], group=(my_g + n + 1) & (G - 1))
        for n in range(G - 1)
    ]
    for copy in y_copies:
        copy.start()

    for drain in drains:
        drain()

    slot = iota((ROWS, HEAD_DIM), 0)
    lines = [jnp.zeros((ROWS, HEAD_DIM), F32)] * STEPS
    for s in range(STEPS):
        for r in range(STAY):
            lines[s] = jnp.where(slot == order[r], result[s * ROWS + r : s * ROWS + r + 1], lines[s])
    for n, copy in enumerate(y_copies):
        copy.wait_recv()
        for s in range(STEPS):
            lines[s] = jnp.where(slot == home[G - 1 - n], y_recv[n, s : s + 1, :], lines[s])
    for copy in y_copies:
        copy.wait_send()
    for s in range(STEPS):
        out_ref[s] = lines[s].astype(BF16)


def per_device(G, C, hidden, cache, lengths, source, target, wq, wkv, qgain, kgain, wo):
    D = hidden.shape[-1]
    BLK = cache.shape[1]
    JJ = C // KV_HEADS
    pieces = C // 8
    half = np.arange(HEAD_DIM // 2, dtype=np.float64)
    freq = (THETA ** (-2.0 * half / HEAD_DIM)).astype(np.float32)
    freq = jnp.asarray(np.concatenate([freq, freq])[None])
    vmem = lambda x: pltpu.VMEM(x.shape, x.dtype)
    smem = lambda x: pltpu.SMEM(x.shape, x.dtype)
    dma = pltpu.SemaphoreType.DMA
    wkv = wkv.T
    operands = (hidden, cache, lengths, source, target, wq, wkv, qgain, kgain, wo, freq)
    return pl.pallas_call(
        functools.partial(kernel, G, C, D, BLK),
        out_shape=jax.ShapeDtypeStruct((STEPS, ROWS, D // C), BF16),
        in_specs=[pl.BlockSpec(memory_space=pltpu.HBM)] * len(operands),
        out_specs=pl.BlockSpec(memory_space=pltpu.VMEM),
        scratch_shapes=[
            vmem(hidden), vmem(cache), vmem(wq), vmem(wkv), vmem(wo), vmem(qgain), vmem(kgain), vmem(freq),
            smem(lengths), smem(source), smem(target),
            pltpu.VMEM((ROWS, 8, HEAD_DIM), F32),
            pltpu.VMEM((G - 1, 8, HEAD_DIM), F32),
            pltpu.VMEM((G - 1, 8, HEAD_DIM), F32),
            pltpu.VMEM((RQ, HEAD_DIM), F32),
            pltpu.VMEM((C, HALF, HEAD_DIM), BF16),
            pltpu.VMEM((C, HALF, HEAD_DIM), BF16),
            pltpu.VMEM((SR, HEAD_DIM), F32),
            pltpu.VMEM((SR, HEAD_DIM), BF16),
            pltpu.VMEM((max(2 * pieces, JJ), SR, HEAD_DIM), BF16),
            pltpu.VMEM((C, HALF, HEAD_DIM), BF16),
            pltpu.VMEM((C, HALF, HEAD_DIM), BF16),
            pltpu.VMEM((C, HALF, HEAD_DIM), BF16),
            pltpu.VMEM((C, HALF, HEAD_DIM), BF16),
            pltpu.VMEM((C, 1, HEAD_DIM), F32),
            pltpu.VMEM((C, 1, HEAD_DIM), F32),
            pltpu.VMEM((RQ, HEAD_DIM), F32),
            pltpu.VMEM((C, SR, D // C), BF16),
            pltpu.VMEM((C, SR, D // C), BF16),
            pltpu.VMEM((G - 1, 8, HEAD_DIM), F32),
            pltpu.VMEM((G - 1, 8, HEAD_DIM), F32),
            dma((9 + CHUNKS,)), dma((ROWS,)), dma((G - 1,)), dma((G - 1,)), dma((2,)), dma((2, KV_HEADS)), dma,
            dma((2 * pieces,)), dma((2,)), dma((2,)), dma, dma, dma, dma, dma((G - 1,)), dma((G - 1,)),
        ],
        compiler_params=pltpu.CompilerParams(
            collective_id=0, has_side_effects=True, vmem_limit_bytes=62 * 1024 * 1024
        ),
    )(*operands)


def solution(mesh):
    in_specs = (
        P(None, "group", None),
        P("group", "ctx", None),
        P(),
        P(),
        P(),
        P(None, "ctx"),
        P(None, "ctx"),
        P(),
        P(),
        P("ctx", None),
    )
    return jax.shard_map(
        functools.partial(per_device, mesh.shape["group"], mesh.shape["ctx"]),
        mesh=mesh, in_specs=in_specs, out_specs=P(None, "group", "ctx"), check_vma=False,
    )
```

```python
import functools
import math

import jax
import jax.numpy as jnp
import numpy as np
from jax import lax
from jax.experimental import pallas as pl
from jax.experimental.pallas import tpu as pltpu
from jax.sharding import PartitionSpec as P

MESH = pl.DeviceIdType.MESH
F32 = jnp.float32
BF16 = jnp.bfloat16

ROWS = 8
STEPS = 2
KV_HEADS = 4
HEAD_DIM = 128
LOCAL_HEADS = 2
Q = LOCAL_HEADS * STEPS
RQ = ROWS * Q
SR = STEPS * ROWS
HALF = RQ // 2
EPS = 1e-6
THETA = 1000000.0
FLOOR = -1e30
LOW = -1e29
FAR_FIRST = (2, 3, 1, 0)
QSCALE = HEAD_DIM**-0.5 * math.log2(math.e)


def iota(shape, dim):
    return lax.broadcasted_iota(jnp.int32, shape, dim)


def pick(order, n):
    if isinstance(n, int):
        return order[n]
    return (sum(v << 2 * k for k, v in enumerate(order)) >> (2 * n)) & 3


def normed(x, gain):
    return x * lax.rsqrt(jnp.mean(x * x, axis=-1, keepdims=True) + EPS) * gain


def rotated(x, cos, sin):
    return x * cos + pltpu.roll(x, HEAD_DIM // 2, 1) * sin


def kernel(
    G, C, D, BLK,
    hidden_h, cache_h, lengths_h, source_h, target_h, wq_h, wkv_h, qgain_h, kgain_h, wo_h, freq_h,
    out_ref,
    hidden, cache, wq, wkv, wo, qgain, kgain, freq, lengths, source, target,
    raw, z_send, z_recv, pre, q_early, q_late, kv_pre, kv_send, kv_recv, a_send, a_recv, ml_send, ml_recv, mix,
    o_send, o_recv, y_send, y_recv,
    load_sem, zs_sem, zr_sem, qs_sem, qr_sem, ks_sem, kr_sem, as_sem, ar_sem, ms_sem, mr_sem,
    os_sem, or_sem, ys_sem, yr_sem,
):
    JJ = C // KV_HEADS
    J_BITS = JJ.bit_length() - 1
    KVW = 2 * KV_HEADS * HEAD_DIM // C
    PIECES = HEAD_DIM // KVW
    STAY = ROWS - (G - 1)
    my_g = lax.axis_index("group")
    my_c = lax.axis_index("ctx")
    my_x = my_c >> J_BITS
    my_low = my_c & (JJ - 1)
    drains = []
    q_all = (q_early, q_late)
    halves = (range(ROWS // 2), range(ROWS // 2, ROWS))

    def neighbour(plane, n):
        y = ((my_low >> 1) ^ pick(FAR_FIRST, n >> 1)) & (JJ // 2 - 1)
        return plane * JJ + y * 2 + ((my_low & 1) ^ (1 - (n & 1)))

    def remote(src, dst, send_sem, recv_sem, **dest):
        return pltpu.make_async_remote_copy(
            src_ref=src, dst_ref=dst, send_sem=send_sem, recv_sem=recv_sem, device_id=dest, device_id_type=MESH
        )

    def bytes_of(ref, sem):
        pltpu.make_async_copy(ref, ref, sem).wait()

    barrier = pltpu.get_barrier_semaphore()
    for n in range(1, G):
        pl.semaphore_signal(barrier, inc=1, device_id={"group": (my_g + n) & (G - 1)}, device_id_type=MESH)

    def greet(n, carry):
        dest = neighbour(my_x ^ pick(FAR_FIRST, n >> J_BITS), n & (JJ - 1))
        pl.semaphore_signal(barrier, inc=1, device_id={"ctx": dest}, device_id_type=MESH)
        return carry

    copies = [(wq_h, wq), (hidden_h, hidden), (wkv_h, wkv), (source_h, source), (target_h, target)]
    copies += [(lengths_h, lengths), (freq_h, freq), (qgain_h, qgain), (kgain_h, kgain)]
    copies += [(cache_h, cache), (wo_h, wo)]
    loads = [pltpu.make_async_copy(a, b, load_sem.at[n]) for n, (a, b) in enumerate(copies)]
    for load in loads[:-2]:
        load.start()
    lax.fori_loop(0, C - 1, greet, 0)

    for load in loads[3:-2]:
        load.wait()
    order = [jnp.int32(0)] * ROWS
    home = [jnp.int32(0)] * G
    listed = [False] * ROWS
    for e in range(source.shape[0]):
        s, t = source[e], target[e]
        off = ((t >> 3) - (s >> 3)) & (G - 1)
        out, back = (s >> 3) == my_g, (t >> 3) == my_g
        for n in range(1, G):
            order[STAY + n - 1] = order[STAY + n - 1] + jnp.where(out & (off == n), s & (ROWS - 1), 0)
            home[n] = home[n] + jnp.where(back & (off == G - n), t & (ROWS - 1), 0)
        for r in range(ROWS):
            listed[r] = listed[r] | (s == my_g * ROWS + r)
    count = jnp.int32(0)
    for r in range(ROWS):
        for n in range(min(r + 1, STAY)):
            order[n] = order[n] + jnp.where((count == n) & jnp.logical_not(listed[r]), r, 0)
        count = count + jnp.where(listed[r], 0, 1)
    row_lengths = [lengths[my_g * ROWS + order[r]] for r in range(ROWS)]

    at, lane = iota((RQ + SR, HEAD_DIM), 0), iota((RQ + SR, HEAD_DIM), 1)
    row = jnp.where(at < RQ, at >> 2, (at - RQ) >> 1)
    position = at & 1
    for r in range(ROWS):
        position = position + jnp.where(row == r, row_lengths[r], 0)
    angle = position.astype(F32) * freq[...]
    cos = jnp.cos(angle)
    sin = jnp.sin(angle)
    sin = jnp.where(lane < HEAD_DIM // 2, -sin, sin)
    q_gain = qgain[...].astype(F32).reshape(1, HEAD_DIM) * QSCALE
    k_gain = kgain[...].astype(F32).reshape(1, HEAD_DIM)

    loads[1].wait()
    loads[2].wait()
    h = jnp.concatenate([hidden[0], hidden[1]], axis=0)
    kv = lax.dot_general(h, wkv[...], (((1,), (1,)), ((), ())), preferred_element_type=F32)
    kv = jnp.concatenate([kv.astype(BF16).astype(F32)] * PIECES, axis=1)
    loads[0].wait()
    for load in loads[-2:]:
        load.start()
    q = jnp.dot(h, wq[...], preferred_element_type=F32).astype(BF16).astype(F32)
    parts = [q[:, j * HEAD_DIM : (j + 1) * HEAD_DIM] for j in range(LOCAL_HEADS)] + [kv]
    for n, x in enumerate(parts):
        for s in range(STEPS):
            raw[:, n * STEPS + s, :] = x[s * ROWS : (s + 1) * ROWS]
    raw[:, Q + STEPS :, :] = jnp.zeros((ROWS, 8 - Q - STEPS, HEAD_DIM), F32)
    for n in range(G - 1):
        z_send[n] = raw[home[n + 1]]

    pl.semaphore_wait(barrier, C - 1 + G - 1)

    for n in range(G - 1):
        remote(z_send.at[n], z_recv.at[n], zs_sem, zr_sem, group=(my_g + n + 1) & (G - 1)).start()
    drains.append(lambda: bytes_of(z_send, zs_sem))

    def send_queries(half):
        rows = slice(half * HALF, (half + 1) * HALF)
        turned = rotated(normed(pre[rows, :], q_gain), cos[rows], sin[rows]).astype(BF16)
        q_all[half][my_c] = turned

        def send_q(n, carry):
            dest = neighbour(my_x ^ pick(FAR_FIRST, n >> J_BITS), n & (JJ - 1))
            remote(
                q_all[half].at[my_c], q_all[half].at[my_c], qs_sem.at[half], qr_sem.at[half], ctx=dest
            ).start()
            return carry

        lax.fori_loop(0, C - 1, send_q, 0)
        drains.append(lambda: bytes_of(q_all[half].at[pl.ds(0, C - 1)], qs_sem.at[half]))
        return turned

    for r in range(STAY):
        pre[r * Q : (r + 1) * Q, :] = raw[order[r], :Q, :]
        kv_pre[r * STEPS : (r + 1) * STEPS, :] = raw[order[r], Q : Q + STEPS, :]
    queries = [send_queries(0)]

    ALL = JJ * HALF
    at, to = iota((ALL, ALL), 0), iota((ALL, ALL), 1)
    to_rows = to == ((at >> 2) & (JJ - 1)) * HALF + (at >> (2 + J_BITS)) * Q + (at & 3)
    to_devices = to == ((at >> 2) & 3) * (JJ * Q) + (at >> 4) * Q + (at & 3)
    to_rows = to_rows.astype(F32).astype(BF16)
    to_devices = to_devices.astype(F32).astype(BF16)
    gather = iota((JJ, 2 * ALL), 0) == ((iota((JJ, 2 * ALL), 1) >> 2) & (JJ - 1))
    gather = gather.astype(F32).astype(BF16)

    bytes_of(z_recv, zr_sem)
    for n in range(1, G):
        r = STAY + n - 1
        pre[r * Q : (r + 1) * Q, :] = z_recv[G - 1 - n, :Q, :]
        kv_pre[r * STEPS : (r + 1) * STEPS, :] = z_recv[G - 1 - n, Q : Q + STEPS, :]
    queries.append(send_queries(1))

    kv_send[...] = kv_pre[...].astype(BF16)
    kv_bits = PIECES.bit_length() - 1
    kv_head = (my_c & (C // 2 - 1)) >> kv_bits
    kv_slot = ((my_c >> (C.bit_length() - 2)) << kv_bits) + (my_c & (PIECES - 1))

    def send_kv(n, carry):
        dest = kv_head * JJ + n

        @pl.when(dest != my_c)
        def _():
            remote(kv_send, kv_recv.at[kv_slot], ks_sem, kr_sem, ctx=dest).start()

        return carry

    lax.fori_loop(0, JJ, send_kv, 0)

    @pl.when(kv_head == my_x)
    def _():
        kv_recv[kv_slot] = kv_send[...]

    def drain_kv():
        @pl.when(kv_head == my_x)
        def _():
            if JJ > 1:
                bytes_of(kv_recv.at[pl.ds(0, JJ - 1)], ks_sem)

        @pl.when(kv_head != my_x)
        def _():
            bytes_of(kv_recv.at[pl.ds(0, JJ)], ks_sem)

    drains.append(drain_kv)

    M = JJ * Q
    place = iota((2 * M, BLK), 1) + my_c * BLK
    lanes = iota((2 * M, HEAD_DIM), 1) - (iota((2 * M, HEAD_DIM), 0) & 3)
    loads[-2].wait()

    def attend(half):
        rows = halves[half]
        send, recv = a_send.at[half], a_recv.at[half]

        bytes_of(q_all[half].at[pl.ds(0, C - 1)], qr_sem.at[half])

        def two_planes(i):
            first = (my_x & 2) ^ (2 - 2 * i)
            nearer = my_x ^ (3 - 2 * i)
            last = my_x ^ (2 - 2 * i)
            k_at = pl.ds(pl.multiple_of(first * HEAD_DIM, 2 * HEAD_DIM), 2 * HEAD_DIM)
            v_at = pl.ds(pl.multiple_of((first + KV_HEADS) * HEAD_DIM, 2 * HEAD_DIM), 2 * HEAD_DIM)
            came = [q_all[half][pl.ds((first + m) * JJ, JJ)].reshape(ALL, HEAD_DIM) for m in range(2)]
            came = [jnp.dot(to_rows, x, preferred_element_type=F32).astype(BF16) for x in came]
            blank = jnp.zeros((M, HEAD_DIM), BF16)
            scores, peaks, weights, totals, sums, high, low = [], [], [], [], [], [], []
            for n, r in enumerate(rows):
                a, b = [x[n * M : (n + 1) * M] for x in came]
                both = jnp.concatenate(
                    [jnp.concatenate([a, blank], axis=1), jnp.concatenate([blank, b], axis=1)], axis=0
                )
                x = lax.dot_general(
                    both, cache[order[r], :, k_at], (((1,), (1,)), ((), ())), preferred_element_type=F32
                )
                scores.append(jnp.where(place < row_lengths[r], x, FLOOR))
            for x in scores:
                peaks.append(jnp.maximum(jnp.max(x, axis=1, keepdims=True), LOW).astype(BF16).astype(F32))
            for x, peak in zip(scores, peaks):
                x = jnp.exp2(x - peak)
                totals.append(jnp.sum(x, axis=1, keepdims=True))
                weights.append(x.astype(BF16))
            for x, r in zip(weights, rows):
                sums.append(jnp.dot(x, cache[order[r], :, v_at], preferred_element_type=F32).astype(BF16))
            for n, (peak, total) in enumerate(zip(peaks, totals)):
                rounded = total.astype(BF16).astype(F32)
                n = rows[n] * Q
                x = jnp.where(lanes == n, peak, jnp.where(lanes == RQ + n, rounded, 0.0))
                high.append(x.astype(BF16))
                low.append(jnp.where(lanes == RQ + n, total - rounded, 0.0).astype(BF16))
            for m in range(2):
                mine = slice(m * M, (m + 1) * M)
                x = jnp.concatenate([x[mine, m * HEAD_DIM : (m + 1) * HEAD_DIM] for x in sums], axis=0)
                x = jnp.dot(to_devices, x, preferred_element_type=F32)
                send[pl.ds((first + m) * JJ, JJ)] = x.astype(BF16).reshape(JJ, HALF, HEAD_DIM)
                x = jnp.concatenate([x[mine] for x in high + low], axis=0)
                x = jnp.dot(gather, x, preferred_element_type=F32)
                if half:
                    x = x + ml_send[pl.ds((first + m) * JJ, JJ), 0, :]
                ml_send[pl.ds((first + m) * JJ, JJ), 0, :] = x

            def send_to(n, carry):
                dest = neighbour(jnp.where((n >= JJ) == (i == 1), last, nearer), n & (JJ - 1))
                remote(send.at[dest], recv.at[my_c], as_sem, ar_sem, ctx=dest).start()
                if half:
                    remote(ml_send.at[dest], ml_recv.at[my_c], ms_sem, mr_sem, ctx=dest).start()

                return carry

            if half:
                for n in range(2 * JJ - i):
                    send_to(n, 0)
            else:
                lax.fori_loop(0, 2 * JJ - i, send_to, 0)

        two_planes(0)
        two_planes(1)
        recv[my_c] = send[my_c]

    attend(0)
    attend(1)
    ml_recv[my_c] = ml_send[my_c]
    drains.append(lambda: bytes_of(a_send.at[:, pl.ds(0, C - 1)], as_sem))
    drains.append(lambda: bytes_of(ml_send.at[pl.ds(0, C - 1)], ms_sem))

    @pl.when(kv_head == my_x)
    def _():
        bytes_of(kv_recv.at[pl.ds(0, 2 * PIECES - 1)], kr_sem)

    @pl.when(kv_head != my_x)
    def _():
        bytes_of(kv_recv.at[pl.ds(0, 2 * PIECES)], kr_sem)

    new = []
    piece = iota((SR, HEAD_DIM), 1) >> (KVW.bit_length() - 1)
    for kind in range(2):
        x = kv_recv[kind * PIECES].astype(F32)
        for n in range(1, PIECES):
            x = jnp.where(piece == n, kv_recv[kind * PIECES + n].astype(F32), x)
        new.append(x)
    new_key = rotated(normed(new[0], k_gain), cos[RQ:], sin[RQ:]).astype(BF16)
    new_value = new[1].astype(BF16)
    q_mine = jnp.concatenate(queries, axis=0)
    scores = lax.dot_general(q_mine, new_key, (((1,), (1,)), ((), ())), preferred_element_type=F32)
    ti, tj = iota(scores.shape, 0), iota(scores.shape, 1)
    scores = jnp.where(((ti >> 2) == (tj >> 1)) & ((tj & 1) <= (ti & 1)), scores, FLOOR)
    new_peak = jnp.max(scores, axis=1, keepdims=True)
    weights = jnp.exp2(scores - new_peak)
    new_total = jnp.sum(weights, axis=1, keepdims=True)
    new_sums = jnp.dot(weights.astype(BF16), new_value, preferred_element_type=F32)

    bytes_of(ml_recv.at[pl.ds(0, C - 1)], mr_sem)
    stats = jnp.transpose(ml_recv[:, 0, :])
    peaks, totals = stats[:RQ], stats[RQ : 2 * RQ]
    highest = jnp.maximum(jnp.max(peaks, axis=1, keepdims=True), new_peak)
    scale = jnp.exp2(peaks - highest)
    new_scale = jnp.exp2(new_peak - highest)
    norm = jnp.sum(scale * totals, axis=1, keepdims=True) + new_scale * new_total
    bytes_of(a_recv.at[:, pl.ds(0, C - 1)], ar_sem)
    for half in range(2):
        rows = slice(half * HALF, (half + 1) * HALF)
        acc = [(new_sums * new_scale)[rows]] + [jnp.zeros((HALF, HEAD_DIM), F32)] * 3
        for n in range(C):
            acc[n & 3] = acc[n & 3] + a_recv[half, n].astype(F32) * scale[rows, n : n + 1]
        mix[rows, :] = ((acc[0] + acc[1]) + (acc[2] + acc[3])) / norm[rows]
    mixed = jnp.concatenate(
        [
            jnp.concatenate([mix[pl.ds(j * STEPS + s, ROWS, stride=Q), :] for s in range(STEPS)], axis=0)
            for j in range(LOCAL_HEADS)
        ],
        axis=1,
    ).astype(BF16)

    loads[-1].wait()
    quarter = D // KV_HEADS
    width = D // C

    for i in range(KV_HEADS):
        g = my_x ^ FAR_FIRST[i]
        part = jnp.dot(
            mixed, wo[:, pl.ds(pl.multiple_of(g * quarter, quarter), quarter)], preferred_element_type=F32
        ).astype(BF16)
        for n in range(JJ):
            o_send[g * JJ + n] = part[:, n * width : (n + 1) * width]
        for n in range(JJ - (FAR_FIRST[i] == 0)):
            dest = neighbour(g, n)
            remote(o_send.at[dest], o_recv.at[my_c], os_sem, or_sem, ctx=dest).start()
    drains.append(lambda: bytes_of(o_send.at[pl.ds(0, C - 1)], os_sem))
    o_recv[my_c] = o_send[my_c]
    bytes_of(o_recv.at[pl.ds(0, C - 1)], or_sem)
    result = jnp.sum(o_recv[...].astype(F32), axis=0)

    for n in range(G - 1):
        for s in range(STEPS):
            y_send[n, s : s + 1, :] = result[s * ROWS + STAY + n : s * ROWS + STAY + n + 1]
        y_send[n, STEPS:, :] = jnp.zeros((8 - STEPS, HEAD_DIM), F32)
    for n in range(G - 1):
        remote(y_send.at[n], y_recv.at[n], ys_sem, yr_sem, group=(my_g + n + 1) & (G - 1)).start()

    for drain in drains:
        drain()

    slot = iota((ROWS, HEAD_DIM), 0)
    lines = [jnp.zeros((ROWS, HEAD_DIM), F32)] * STEPS
    for s in range(STEPS):
        for r in range(STAY):
            lines[s] = jnp.where(slot == order[r], result[s * ROWS + r : s * ROWS + r + 1], lines[s])
    bytes_of(y_recv, yr_sem)
    for n in range(G - 1):
        for s in range(STEPS):
            lines[s] = jnp.where(slot == home[G - 1 - n], y_recv[n, s : s + 1, :], lines[s])
    bytes_of(y_send, ys_sem)
    for s in range(STEPS):
        out_ref[s] = lines[s].astype(BF16)


def per_device(G, C, hidden, cache, lengths, source, target, wq, wkv, qgain, kgain, wo):
    D = hidden.shape[-1]
    BLK = cache.shape[1]
    JJ = C // KV_HEADS
    pieces = C // 8
    half = np.arange(HEAD_DIM // 2, dtype=np.float64)
    freq = (THETA ** (-2.0 * half / HEAD_DIM)).astype(np.float32)
    freq = jnp.asarray(np.concatenate([freq, freq])[None])
    vmem = lambda x: pltpu.VMEM(x.shape, x.dtype)
    smem = lambda x: pltpu.SMEM(x.shape, x.dtype)
    dma = pltpu.SemaphoreType.DMA
    wkv = wkv.T
    operands = (hidden, cache, lengths, source, target, wq, wkv, qgain, kgain, wo, freq)
    return pl.pallas_call(
        functools.partial(kernel, G, C, D, BLK),
        out_shape=jax.ShapeDtypeStruct((STEPS, ROWS, D // C), BF16),
        in_specs=[pl.BlockSpec(memory_space=pltpu.HBM)] * len(operands),
        out_specs=pl.BlockSpec(memory_space=pltpu.VMEM),
        scratch_shapes=[
            vmem(hidden), vmem(cache), vmem(wq), vmem(wkv), vmem(wo), vmem(qgain), vmem(kgain), vmem(freq),
            smem(lengths), smem(source), smem(target),
            pltpu.VMEM((ROWS, 8, HEAD_DIM), F32),
            pltpu.VMEM((G - 1, 8, HEAD_DIM), F32),
            pltpu.VMEM((G - 1, 8, HEAD_DIM), F32),
            pltpu.VMEM((RQ, HEAD_DIM), F32),
            pltpu.VMEM((C, HALF, HEAD_DIM), BF16),
            pltpu.VMEM((C, HALF, HEAD_DIM), BF16),
            pltpu.VMEM((SR, HEAD_DIM), F32),
            pltpu.VMEM((SR, HEAD_DIM), BF16),
            pltpu.VMEM((max(2 * pieces, JJ), SR, HEAD_DIM), BF16),
            pltpu.VMEM((2, C, HALF, HEAD_DIM), BF16),
            pltpu.VMEM((2, C, HALF, HEAD_DIM), BF16),
            pltpu.VMEM((C, 1, HEAD_DIM), F32),
            pltpu.VMEM((C, 1, HEAD_DIM), F32),
            pltpu.VMEM((RQ, HEAD_DIM), F32),
            pltpu.VMEM((C, SR, D // C), BF16),
            pltpu.VMEM((C, SR, D // C), BF16),
            pltpu.VMEM((G - 1, 8, HEAD_DIM), F32),
            pltpu.VMEM((G - 1, 8, HEAD_DIM), F32),
            dma((11,)), dma, dma, dma((2,)), dma((2,)), dma, dma, dma, dma, dma, dma, dma, dma, dma, dma,
        ],
        compiler_params=pltpu.CompilerParams(
            collective_id=0, has_side_effects=True, vmem_limit_bytes=62 * 1024 * 1024
        ),
    )(*operands)


def solution(mesh):
    in_specs = (
        P(None, "group", None),
        P("group", "ctx", None),
        P(),
        P(),
        P(),
        P(None, "ctx"),
        P(None, "ctx"),
        P(),
        P(),
        P("ctx", None),
    )
    return jax.shard_map(
        functools.partial(per_device, mesh.shape["group"], mesh.shape["ctx"]),
        mesh=mesh, in_specs=in_specs, out_specs=P(None, "group", "ctx"), check_vma=False,
    )
```

```python
import functools
import math

import jax
import jax.numpy as jnp
import numpy as np
from jax import lax
from jax.experimental import pallas as pl
from jax.experimental.pallas import tpu as pltpu
from jax.sharding import PartitionSpec as P

MESH = pl.DeviceIdType.MESH
F32 = jnp.float32
BF16 = jnp.bfloat16

ROWS = 8
STEPS = 2
KV_HEADS = 4
HEAD_DIM = 128
LOCAL_HEADS = 2
Q = LOCAL_HEADS * STEPS
RQ = ROWS * Q
SR = STEPS * ROWS
HALF = RQ // 2
EPS = 1e-6
THETA = 1000000.0
FLOOR = -1e30
LOW = -1e29
FAR_FIRST = (2, 3, 1, 0)
QSCALE = HEAD_DIM**-0.5 * math.log2(math.e)


def iota(shape, dim):
    return lax.broadcasted_iota(jnp.int32, shape, dim)


def pick(order, n):
    if isinstance(n, int):
        return order[n]
    return (sum(v << 2 * k for k, v in enumerate(order)) >> (2 * n)) & 3


def normed(x, gain):
    return x * lax.rsqrt(jnp.mean(x * x, axis=-1, keepdims=True) + EPS) * gain


def rotated(x, cos, sin):
    return x * cos + pltpu.roll(x, HEAD_DIM // 2, 1) * sin


def kernel(
    G, C, D, BLK,
    hidden_h, cache_h, lengths_h, source_h, target_h, wq_h, wkv_h, qgain_h, kgain_h, wo_h, freq_h,
    out_ref,
    hidden, cache, wq, wkv, wo, qgain, kgain, freq, lengths, source, target,
    raw, z_send, z_recv, pre, q_early, q_late, turned_keys, kv_pre, kv_send, kv_recv, a_send, a_recv, ml_send, ml_recv, mix,
    o_send, o_recv, y_send, y_recv,
    load_sem, zs_sem, zr_sem, qs_sem, qr_sem, ks_sem, kr_sem, as_sem, ar_sem, ms_sem, mr_sem,
    os_sem, or_sem, ys_sem, yr_sem,
):
    JJ = C // KV_HEADS
    J_BITS = JJ.bit_length() - 1
    KVW = 2 * KV_HEADS * HEAD_DIM // C
    PIECES = HEAD_DIM // KVW
    STAY = ROWS - (G - 1)
    my_g = lax.axis_index("group")
    my_c = lax.axis_index("ctx")
    my_x = my_c >> J_BITS
    my_low = my_c & (JJ - 1)
    drains = []
    q_all = (q_early, q_late)
    halves = (range(ROWS // 2), range(ROWS // 2, ROWS))

    def neighbour(plane, n):
        y = ((my_low >> 1) ^ pick(FAR_FIRST, n >> 1)) & (JJ // 2 - 1)
        return plane * JJ + y * 2 + ((my_low & 1) ^ (1 - (n & 1)))

    def remote(src, dst, send_sem, recv_sem, **dest):
        return pltpu.make_async_remote_copy(
            src_ref=src, dst_ref=dst, send_sem=send_sem, recv_sem=recv_sem, device_id=dest, device_id_type=MESH
        )

    def bytes_of(ref, sem):
        pltpu.make_async_copy(ref, ref, sem).wait()

    barrier = pltpu.get_barrier_semaphore()
    for n in range(1, G):
        pl.semaphore_signal(barrier, inc=1, device_id={"group": (my_g + n) & (G - 1)}, device_id_type=MESH)

    def greet(n, carry):
        dest = neighbour(my_x ^ pick(FAR_FIRST, n >> J_BITS), n & (JJ - 1))
        pl.semaphore_signal(barrier, inc=1, device_id={"ctx": dest}, device_id_type=MESH)
        return carry

    copies = [(wq_h, wq), (hidden_h, hidden), (wkv_h, wkv), (source_h, source), (target_h, target)]
    copies += [(lengths_h, lengths), (freq_h, freq), (qgain_h, qgain), (kgain_h, kgain)]
    copies += [(cache_h, cache), (wo_h, wo)]
    loads = [pltpu.make_async_copy(a, b, load_sem.at[n]) for n, (a, b) in enumerate(copies)]
    for load in loads[:3]:
        load.start()
    lax.fori_loop(0, C - 1, greet, 0)
    for load in loads[3:-2]:
        load.start()

    for load in loads[3:-2]:
        load.wait()
    order = [jnp.int32(0)] * ROWS
    home = [jnp.int32(0)] * G
    listed = [False] * ROWS
    for e in range(source.shape[0]):
        s, t = source[e], target[e]
        off = ((t >> 3) - (s >> 3)) & (G - 1)
        out, back = (s >> 3) == my_g, (t >> 3) == my_g
        for n in range(1, G):
            order[STAY + n - 1] = order[STAY + n - 1] + jnp.where(out & (off == n), s & (ROWS - 1), 0)
            home[n] = home[n] + jnp.where(back & (off == G - n), t & (ROWS - 1), 0)
        for r in range(ROWS):
            listed[r] = listed[r] | (s == my_g * ROWS + r)
    count = jnp.int32(0)
    for r in range(ROWS):
        for n in range(min(r + 1, STAY)):
            order[n] = order[n] + jnp.where((count == n) & jnp.logical_not(listed[r]), r, 0)
        count = count + jnp.where(listed[r], 0, 1)
    row_lengths = [lengths[my_g * ROWS + order[r]] for r in range(ROWS)]

    loads[1].wait()
    loads[2].wait()
    h = jnp.concatenate([hidden[0], hidden[1]], axis=0)
    kv = lax.dot_general(h, wkv[...], (((1,), (1,)), ((), ())), preferred_element_type=F32)
    kv = jnp.concatenate([kv.astype(BF16).astype(F32)] * PIECES, axis=1)
    loads[0].wait()
    for load in loads[-2:]:
        load.start()
    q = jnp.dot(h, wq[...], preferred_element_type=F32).astype(BF16).astype(F32)
    parts = [q[:, j * HEAD_DIM : (j + 1) * HEAD_DIM] for j in range(LOCAL_HEADS)] + [kv]
    for n, x in enumerate(parts):
        for s in range(STEPS):
            raw[:, n * STEPS + s, :] = x[s * ROWS : (s + 1) * ROWS]
    raw[:, Q + STEPS :, :] = jnp.zeros((ROWS, 8 - Q - STEPS, HEAD_DIM), F32)
    for n in range(G - 1):
        z_send[n] = raw[home[n + 1]]

    pl.semaphore_wait(barrier, C - 1 + G - 1)

    for n in range(G - 1):
        remote(z_send.at[n], z_recv.at[n], zs_sem, zr_sem, group=(my_g + n + 1) & (G - 1)).start()
    drains.append(lambda: bytes_of(z_send, zs_sem))

    at, lane = iota((RQ + SR, HEAD_DIM), 0), iota((RQ + SR, HEAD_DIM), 1)
    row = jnp.where(at < RQ, at >> 2, (at - RQ) >> 1)
    position = at & 1
    for r in range(ROWS):
        position = position + jnp.where(row == r, row_lengths[r], 0)
    angle = position.astype(F32) * freq[...]
    cos = jnp.cos(angle)
    sin = jnp.sin(angle)
    sin = jnp.where(lane < HEAD_DIM // 2, -sin, sin)
    q_gain = qgain[...].astype(F32).reshape(1, HEAD_DIM) * QSCALE
    k_gain = kgain[...].astype(F32).reshape(1, HEAD_DIM)

    def send_queries(half):
        rows = slice(half * HALF, (half + 1) * HALF)
        turned = rotated(normed(pre[rows, :], q_gain), cos[rows], sin[rows]).astype(BF16)
        q_all[half][my_c] = turned

        def send_q(n, carry):
            dest = neighbour(my_x ^ pick(FAR_FIRST, n >> J_BITS), n & (JJ - 1))
            remote(
                q_all[half].at[my_c], q_all[half].at[my_c], qs_sem.at[half], qr_sem.at[half], ctx=dest
            ).start()
            return carry

        lax.fori_loop(0, C - 1, send_q, 0)
        drains.append(lambda: bytes_of(q_all[half].at[pl.ds(0, C - 1)], qs_sem.at[half]))
        return turned

    for r in range(STAY):
        pre[r * Q : (r + 1) * Q, :] = raw[order[r], :Q, :]
        kv_pre[r * STEPS : (r + 1) * STEPS, :] = raw[order[r], Q : Q + STEPS, :]
    queries = [send_queries(0)]

    ALL = JJ * HALF
    at, to = iota((ALL, ALL), 0), iota((ALL, ALL), 1)
    to_rows = to == ((at >> 2) & (JJ - 1)) * HALF + (at >> (2 + J_BITS)) * Q + (at & 3)
    to_devices = to == ((at >> 2) & 3) * (JJ * Q) + (at >> 4) * Q + (at & 3)
    to_rows = to_rows.astype(F32).astype(BF16)
    to_devices = to_devices.astype(F32).astype(BF16)
    gather = iota((JJ, 2 * ALL), 0) == ((iota((JJ, 2 * ALL), 1) >> 2) & (JJ - 1))
    gather = gather.astype(F32).astype(BF16)

    bytes_of(z_recv, zr_sem)
    for n in range(1, G):
        r = STAY + n - 1
        pre[r * Q : (r + 1) * Q, :] = z_recv[G - 1 - n, :Q, :]
        kv_pre[r * STEPS : (r + 1) * STEPS, :] = z_recv[G - 1 - n, Q : Q + STEPS, :]
    queries.append(send_queries(1))

    kv_send[...] = kv_pre[...].astype(BF16)
    kv_bits = PIECES.bit_length() - 1
    kv_head = (my_c & (C // 2 - 1)) >> kv_bits
    kv_slot = ((my_c >> (C.bit_length() - 2)) << kv_bits) + (my_c & (PIECES - 1))

    def send_kv(n, carry):
        dest = kv_head * JJ + n

        @pl.when(dest != my_c)
        def _():
            remote(kv_send, kv_recv.at[kv_slot], ks_sem, kr_sem, ctx=dest).start()

        return carry

    lax.fori_loop(0, JJ, send_kv, 0)

    @pl.when(kv_head == my_x)
    def _():
        kv_recv[kv_slot] = kv_send[...]

    def drain_kv():
        @pl.when(kv_head == my_x)
        def _():
            if JJ > 1:
                bytes_of(kv_recv.at[pl.ds(0, JJ - 1)], ks_sem)

        @pl.when(kv_head != my_x)
        def _():
            bytes_of(kv_recv.at[pl.ds(0, JJ)], ks_sem)

    drains.append(drain_kv)

    M = JJ * Q
    place = iota((2 * M, BLK), 1) + my_c * BLK
    lanes = iota((2 * M, HEAD_DIM), 1) - (iota((2 * M, HEAD_DIM), 0) & 3)
    loads[-2].wait()

    PAIR = 2 * HEAD_DIM
    unit = (iota((PAIR, PAIR), 0) == iota((PAIR, PAIR), 1)).astype(F32).astype(BF16)
    for n, r in enumerate(halves[1]):
        for k in range(KV_HEADS // 2):
            at = slice(k * PAIR, (k + 1) * PAIR)
            x = lax.dot_general(
                unit, cache[order[r], :, at], (((1,), (1,)), ((), ())), preferred_element_type=F32
            )
            turned_keys[n, at, :] = x.astype(BF16)

    def attend(half):
        rows = halves[half]
        send, recv = a_send.at[half], a_recv.at[half]

        bytes_of(q_all[half].at[pl.ds(0, C - 1)], qr_sem.at[half])

        def two_planes(i):
            first = (my_x & 2) ^ (2 - 2 * i)
            nearer = my_x ^ (3 - 2 * i)
            last = my_x ^ (2 - 2 * i)
            k_at = pl.ds(pl.multiple_of(first * HEAD_DIM, 2 * HEAD_DIM), 2 * HEAD_DIM)
            v_at = pl.ds(pl.multiple_of((first + KV_HEADS) * HEAD_DIM, 2 * HEAD_DIM), 2 * HEAD_DIM)
            came = [q_all[half][pl.ds((first + m) * JJ, JJ)].reshape(ALL, HEAD_DIM) for m in range(2)]
            came = [jnp.dot(to_rows, x, preferred_element_type=F32).astype(BF16) for x in came]
            blank = jnp.zeros((M, HEAD_DIM), BF16)
            scores, peaks, weights, totals, sums, high, low = [], [], [], [], [], [], []
            for n, r in enumerate(rows):
                a, b = [x[n * M : (n + 1) * M] for x in came]
                both = jnp.concatenate(
                    [jnp.concatenate([a, blank], axis=1), jnp.concatenate([blank, b], axis=1)], axis=0
                )
                if half:
                    x = jnp.dot(both, turned_keys[n, k_at, :], preferred_element_type=F32)
                else:
                    x = lax.dot_general(
                        both, cache[order[r], :, k_at], (((1,), (1,)), ((), ())), preferred_element_type=F32
                    )
                scores.append(jnp.where(place < row_lengths[r], x, FLOOR))
            for x in scores:
                peaks.append(jnp.maximum(jnp.max(x, axis=1, keepdims=True), LOW).astype(BF16).astype(F32))
            for x, peak in zip(scores, peaks):
                x = jnp.exp2(x - peak)
                totals.append(jnp.sum(x, axis=1, keepdims=True))
                weights.append(x.astype(BF16))
            for x, r in zip(weights, rows):
                sums.append(jnp.dot(x, cache[order[r], :, v_at], preferred_element_type=F32).astype(BF16))
            for n, (peak, total) in enumerate(zip(peaks, totals)):
                rounded = total.astype(BF16).astype(F32)
                n = rows[n] * Q
                x = jnp.where(lanes == n, peak, jnp.where(lanes == RQ + n, rounded, 0.0))
                high.append(x.astype(BF16))
                low.append(jnp.where(lanes == RQ + n, total - rounded, 0.0).astype(BF16))
            for m in range(2):
                mine = slice(m * M, (m + 1) * M)
                x = jnp.concatenate([x[mine, m * HEAD_DIM : (m + 1) * HEAD_DIM] for x in sums], axis=0)
                x = jnp.dot(to_devices, x, preferred_element_type=F32)
                send[pl.ds((first + m) * JJ, JJ)] = x.astype(BF16).reshape(JJ, HALF, HEAD_DIM)
                x = jnp.concatenate([x[mine] for x in high + low], axis=0)
                x = jnp.dot(gather, x, preferred_element_type=F32)
                if half:
                    x = x + ml_send[pl.ds((first + m) * JJ, JJ), 0, :]
                ml_send[pl.ds((first + m) * JJ, JJ), 0, :] = x

            def send_to(n, carry):
                dest = neighbour(jnp.where((n >= JJ) == (i == 1), last, nearer), n & (JJ - 1))
                remote(send.at[dest], recv.at[my_c], as_sem, ar_sem, ctx=dest).start()
                if half:
                    remote(ml_send.at[dest], ml_recv.at[my_c], ms_sem, mr_sem, ctx=dest).start()

                return carry

            if half:
                turns = range(2 * JJ - i)
                if JJ == 8:
                    turns = (0, 1, 8, 9, 2, 3, 4, 5, 10, 11, 12, 13, 6, 7, 14, 15)[: 2 * JJ - i]
                for n in turns:
                    send_to(n, 0)
            else:
                lax.fori_loop(0, 2 * JJ - i, send_to, 0)

        two_planes(0)
        two_planes(1)
        recv[my_c] = send[my_c]

    attend(0)
    attend(1)
    ml_recv[my_c] = ml_send[my_c]
    drains.append(lambda: bytes_of(a_send.at[:, pl.ds(0, C - 1)], as_sem))
    drains.append(lambda: bytes_of(ml_send.at[pl.ds(0, C - 1)], ms_sem))

    @pl.when(kv_head == my_x)
    def _():
        bytes_of(kv_recv.at[pl.ds(0, 2 * PIECES - 1)], kr_sem)

    @pl.when(kv_head != my_x)
    def _():
        bytes_of(kv_recv.at[pl.ds(0, 2 * PIECES)], kr_sem)

    new = []
    piece = iota((SR, HEAD_DIM), 1) >> (KVW.bit_length() - 1)
    for kind in range(2):
        x = kv_recv[kind * PIECES].astype(F32)
        for n in range(1, PIECES):
            x = jnp.where(piece == n, kv_recv[kind * PIECES + n].astype(F32), x)
        new.append(x)
    new_key = rotated(normed(new[0], k_gain), cos[RQ:], sin[RQ:]).astype(BF16)
    new_value = new[1].astype(BF16)
    q_mine = jnp.concatenate(queries, axis=0)
    scores = lax.dot_general(q_mine, new_key, (((1,), (1,)), ((), ())), preferred_element_type=F32)
    ti, tj = iota(scores.shape, 0), iota(scores.shape, 1)
    scores = jnp.where(((ti >> 2) == (tj >> 1)) & ((tj & 1) <= (ti & 1)), scores, FLOOR)
    new_peak = jnp.max(scores, axis=1, keepdims=True)
    weights = jnp.exp2(scores - new_peak)
    new_total = jnp.sum(weights, axis=1, keepdims=True)
    new_sums = jnp.dot(weights.astype(BF16), new_value, preferred_element_type=F32)

    bytes_of(ml_recv.at[pl.ds(0, C - 1)], mr_sem)
    stats = jnp.transpose(ml_recv[:, 0, :])
    peaks, totals = stats[:RQ], stats[RQ : 2 * RQ]
    highest = jnp.maximum(jnp.max(peaks, axis=1, keepdims=True), new_peak)
    scale = jnp.exp2(peaks - highest)
    new_scale = jnp.exp2(new_peak - highest)
    norm = jnp.sum(scale * totals, axis=1, keepdims=True) + new_scale * new_total
    bytes_of(a_recv.at[:, pl.ds(0, C - 1)], ar_sem)
    for half in range(2):
        rows = slice(half * HALF, (half + 1) * HALF)
        acc = [(new_sums * new_scale)[rows]] + [jnp.zeros((HALF, HEAD_DIM), F32)] * 3
        for n in range(C):
            acc[n & 3] = acc[n & 3] + a_recv[half, n].astype(F32) * scale[rows, n : n + 1]
        mix[rows, :] = ((acc[0] + acc[1]) + (acc[2] + acc[3])) / norm[rows]
    mixed = jnp.concatenate(
        [
            jnp.concatenate([mix[pl.ds(j * STEPS + s, ROWS, stride=Q), :] for s in range(STEPS)], axis=0)
            for j in range(LOCAL_HEADS)
        ],
        axis=1,
    ).astype(BF16)

    loads[-1].wait()
    quarter = D // KV_HEADS
    width = D // C

    for i in range(KV_HEADS):
        g = my_x ^ FAR_FIRST[i]
        part = jnp.dot(
            mixed, wo[:, pl.ds(pl.multiple_of(g * quarter, quarter), quarter)], preferred_element_type=F32
        ).astype(BF16)
        for n in range(JJ):
            o_send[g * JJ + n] = part[:, n * width : (n + 1) * width]
        if i == 1:
            turns = [(0, n) for n in range(JJ)] + [(1, n) for n in range(JJ)]
        elif i == 3:
            turns = [(2, n) for n in range(JJ)] + [(3, n) for n in range(JJ - 1)]
            if JJ == 8:
                turns = [turns[n] for n in (0, 1, 8, 9, 2, 3, 4, 5, 10, 11, 12, 13, 6, 7, 14)]
        else:
            turns = []
        for a, n in turns:
            dest = neighbour(my_x ^ FAR_FIRST[a], n)
            remote(o_send.at[dest], o_recv.at[my_c], os_sem, or_sem, ctx=dest).start()
    drains.append(lambda: bytes_of(o_send.at[pl.ds(0, C - 1)], os_sem))
    o_recv[my_c] = o_send[my_c]
    bytes_of(o_recv.at[pl.ds(0, C - 1)], or_sem)
    result = jnp.sum(o_recv[...].astype(F32), axis=0)

    for n in range(G - 1):
        for s in range(STEPS):
            y_send[n, s : s + 1, :] = result[s * ROWS + STAY + n : s * ROWS + STAY + n + 1]
        y_send[n, STEPS:, :] = jnp.zeros((8 - STEPS, HEAD_DIM), F32)
    for n in range(G - 1):
        remote(y_send.at[n], y_recv.at[n], ys_sem, yr_sem, group=(my_g + n + 1) & (G - 1)).start()

    for drain in drains:
        drain()

    slot = iota((ROWS, HEAD_DIM), 0)
    lines = [jnp.zeros((ROWS, HEAD_DIM), F32)] * STEPS
    for s in range(STEPS):
        for r in range(STAY):
            lines[s] = jnp.where(slot == order[r], result[s * ROWS + r : s * ROWS + r + 1], lines[s])
    bytes_of(y_recv, yr_sem)
    for n in range(G - 1):
        for s in range(STEPS):
            lines[s] = jnp.where(slot == home[G - 1 - n], y_recv[n, s : s + 1, :], lines[s])
    bytes_of(y_send, ys_sem)
    for s in range(STEPS):
        out_ref[s] = lines[s].astype(BF16)


def per_device(G, C, hidden, cache, lengths, source, target, wq, wkv, qgain, kgain, wo):
    D = hidden.shape[-1]
    BLK = cache.shape[1]
    JJ = C // KV_HEADS
    pieces = C // 8
    half = np.arange(HEAD_DIM // 2, dtype=np.float64)
    freq = (THETA ** (-2.0 * half / HEAD_DIM)).astype(np.float32)
    freq = jnp.asarray(np.concatenate([freq, freq])[None])
    vmem = lambda x: pltpu.VMEM(x.shape, x.dtype)
    smem = lambda x: pltpu.SMEM(x.shape, x.dtype)
    dma = pltpu.SemaphoreType.DMA
    wkv = wkv.T
    operands = (hidden, cache, lengths, source, target, wq, wkv, qgain, kgain, wo, freq)
    return pl.pallas_call(
        functools.partial(kernel, G, C, D, BLK),
        out_shape=jax.ShapeDtypeStruct((STEPS, ROWS, D // C), BF16),
        in_specs=[pl.BlockSpec(memory_space=pltpu.HBM)] * len(operands),
        out_specs=pl.BlockSpec(memory_space=pltpu.VMEM),
        scratch_shapes=[
            vmem(hidden), vmem(cache), vmem(wq), vmem(wkv), vmem(wo), vmem(qgain), vmem(kgain), vmem(freq),
            smem(lengths), smem(source), smem(target),
            pltpu.VMEM((ROWS, 8, HEAD_DIM), F32),
            pltpu.VMEM((G - 1, 8, HEAD_DIM), F32),
            pltpu.VMEM((G - 1, 8, HEAD_DIM), F32),
            pltpu.VMEM((RQ, HEAD_DIM), F32),
            pltpu.VMEM((C, HALF, HEAD_DIM), BF16),
            pltpu.VMEM((C, HALF, HEAD_DIM), BF16),
            pltpu.VMEM((ROWS // 2, KV_HEADS * HEAD_DIM, BLK), BF16),
            pltpu.VMEM((SR, HEAD_DIM), F32),
            pltpu.VMEM((SR, HEAD_DIM), BF16),
            pltpu.VMEM((max(2 * pieces, JJ), SR, HEAD_DIM), BF16),
            pltpu.VMEM((2, C, HALF, HEAD_DIM), BF16),
            pltpu.VMEM((2, C, HALF, HEAD_DIM), BF16),
            pltpu.VMEM((C, 1, HEAD_DIM), F32),
            pltpu.VMEM((C, 1, HEAD_DIM), F32),
            pltpu.VMEM((RQ, HEAD_DIM), F32),
            pltpu.VMEM((C, SR, D // C), BF16),
            pltpu.VMEM((C, SR, D // C), BF16),
            pltpu.VMEM((G - 1, 8, HEAD_DIM), F32),
            pltpu.VMEM((G - 1, 8, HEAD_DIM), F32),
            dma((11,)), dma, dma, dma((2,)), dma((2,)), dma, dma, dma, dma, dma, dma, dma, dma, dma, dma,
        ],
        compiler_params=pltpu.CompilerParams(
            collective_id=0, has_side_effects=True, vmem_limit_bytes=62 * 1024 * 1024
        ),
    )(*operands)


def solution(mesh):
    in_specs = (
        P(None, "group", None),
        P("group", "ctx", None),
        P(),
        P(),
        P(),
        P(None, "ctx"),
        P(None, "ctx"),
        P(),
        P(),
        P("ctx", None),
    )
    return jax.shard_map(
        functools.partial(per_device, mesh.shape["group"], mesh.shape["ctx"]),
        mesh=mesh, in_specs=in_specs, out_specs=P(None, "group", "ctx"), check_vma=False,
    )
```

```python
import functools
import math

import jax
import jax.numpy as jnp
import numpy as np
from jax import lax
from jax.experimental import pallas as pl
from jax.experimental.pallas import tpu as pltpu
from jax.sharding import PartitionSpec as P

MESH = pl.DeviceIdType.MESH
F32 = jnp.float32
BF16 = jnp.bfloat16

ROWS = 8
STEPS = 2
KV_HEADS = 4
HEAD_DIM = 128
LOCAL_HEADS = 2
Q = LOCAL_HEADS * STEPS
RQ = ROWS * Q
SR = STEPS * ROWS
HALF = RQ // 2
EPS = 1e-6
THETA = 1000000.0
FLOOR = -1e30
LOW = -1e29
FAR_FIRST = (2, 3, 1, 0)
QSCALE = HEAD_DIM**-0.5 * math.log2(math.e)


def iota(shape, dim):
    return lax.broadcasted_iota(jnp.int32, shape, dim)


def pick(order, n):
    if isinstance(n, int):
        return order[n]
    return (sum(v << 2 * k for k, v in enumerate(order)) >> (2 * n)) & 3


def normed(x, gain):
    return x * lax.rsqrt(jnp.mean(x * x, axis=-1, keepdims=True) + EPS) * gain


def rotated(x, cos, sin):
    return x * cos + pltpu.roll(x, HEAD_DIM // 2, 1) * sin


def kernel(
    G, C, D, BLK,
    hidden_h, cache_h, lengths_h, source_h, target_h, wq_h, wkv_h, qgain_h, kgain_h, wo_h, freq_h,
    out_ref,
    hidden, cache, wq, wkv, wo, qgain, kgain, freq, lengths, source, target,
    raw, z_send, z_recv, pre, q_early, q_late, turned_keys, kv_pre, kv_send, kv_recv, a_send, a_recv, ml_send, ml_recv, spread, mix,
    o_send, o_recv, y_send, y_recv,
    load_sem, zs_sem, zr_sem, qs_sem, qr_sem, ks_sem, kr_sem, as_sem, ar_sem, ms_sem, mr_sem,
    os_sem, or_sem, ys_sem, yr_sem,
):
    JJ = C // KV_HEADS
    J_BITS = JJ.bit_length() - 1
    KVW = 2 * KV_HEADS * HEAD_DIM // C
    PIECES = HEAD_DIM // KVW
    STAY = ROWS - (G - 1)
    my_g = lax.axis_index("group")
    my_c = lax.axis_index("ctx")
    my_x = my_c >> J_BITS
    my_low = my_c & (JJ - 1)
    drains = []
    q_all = (q_early, q_late)
    halves = (range(ROWS // 2), range(ROWS // 2, ROWS))

    def neighbour(plane, n):
        y = ((my_low >> 1) ^ pick(FAR_FIRST, n >> 1)) & (JJ // 2 - 1)
        return plane * JJ + y * 2 + ((my_low & 1) ^ (1 - (n & 1)))

    def remote(src, dst, send_sem, recv_sem, **dest):
        return pltpu.make_async_remote_copy(
            src_ref=src, dst_ref=dst, send_sem=send_sem, recv_sem=recv_sem, device_id=dest, device_id_type=MESH
        )

    def bytes_of(ref, sem):
        pltpu.make_async_copy(ref, ref, sem).wait()

    barrier = pltpu.get_barrier_semaphore()
    for n in range(1, G):
        pl.semaphore_signal(barrier, inc=1, device_id={"group": (my_g + n) & (G - 1)}, device_id_type=MESH)

    def greet(n, carry):
        dest = neighbour(my_x ^ pick(FAR_FIRST, n >> J_BITS), n & (JJ - 1))
        pl.semaphore_signal(barrier, inc=1, device_id={"ctx": dest}, device_id_type=MESH)
        return carry

    copies = [(wq_h, wq), (hidden_h, hidden), (wkv_h, wkv), (source_h, source), (target_h, target)]
    copies += [(lengths_h, lengths), (freq_h, freq), (qgain_h, qgain), (kgain_h, kgain)]
    copies += [(cache_h, cache), (wo_h, wo)]
    loads = [pltpu.make_async_copy(a, b, load_sem.at[n]) for n, (a, b) in enumerate(copies)]
    for load in loads[:3]:
        load.start()
    lax.fori_loop(0, C - 1, greet, 0)
    for load in loads[3:-2]:
        load.start()

    for load in loads[3:-2]:
        load.wait()
    order = [jnp.int32(0)] * ROWS
    home = [jnp.int32(0)] * G
    listed = [False] * ROWS
    for e in range(source.shape[0]):
        s, t = source[e], target[e]
        off = ((t >> 3) - (s >> 3)) & (G - 1)
        out, back = (s >> 3) == my_g, (t >> 3) == my_g
        for n in range(1, G):
            order[STAY + n - 1] = order[STAY + n - 1] + jnp.where(out & (off == n), s & (ROWS - 1), 0)
            home[n] = home[n] + jnp.where(back & (off == G - n), t & (ROWS - 1), 0)
        for r in range(ROWS):
            listed[r] = listed[r] | (s == my_g * ROWS + r)
    count = jnp.int32(0)
    for r in range(ROWS):
        for n in range(min(r + 1, STAY)):
            order[n] = order[n] + jnp.where((count == n) & jnp.logical_not(listed[r]), r, 0)
        count = count + jnp.where(listed[r], 0, 1)
    row_lengths = [lengths[my_g * ROWS + order[r]] for r in range(ROWS)]

    loads[1].wait()
    loads[2].wait()
    h = jnp.concatenate([hidden[0], hidden[1]], axis=0)
    kv = lax.dot_general(h, wkv[...], (((1,), (1,)), ((), ())), preferred_element_type=F32)
    kv = jnp.concatenate([kv.astype(BF16).astype(F32)] * PIECES, axis=1)
    loads[0].wait()
    for load in loads[-2:]:
        load.start()
    q = jnp.dot(h, wq[...], preferred_element_type=F32).astype(BF16).astype(F32)
    parts = [q[:, j * HEAD_DIM : (j + 1) * HEAD_DIM] for j in range(LOCAL_HEADS)] + [kv]
    for n, x in enumerate(parts):
        for s in range(STEPS):
            raw[:, n * STEPS + s, :] = x[s * ROWS : (s + 1) * ROWS]
    raw[:, Q + STEPS :, :] = jnp.zeros((ROWS, 8 - Q - STEPS, HEAD_DIM), F32)
    for n in range(G - 1):
        z_send[n] = raw[home[n + 1]]

    pl.semaphore_wait(barrier, C - 1 + G - 1)

    for n in range(G - 1):
        remote(z_send.at[n], z_recv.at[n], zs_sem, zr_sem, group=(my_g + n + 1) & (G - 1)).start()
    drains.append(lambda: bytes_of(z_send, zs_sem))

    at, lane = iota((RQ + SR, HEAD_DIM), 0), iota((RQ + SR, HEAD_DIM), 1)
    row = jnp.where(at < RQ, at >> 2, (at - RQ) >> 1)
    position = at & 1
    for r in range(ROWS):
        position = position + jnp.where(row == r, row_lengths[r], 0)
    angle = position.astype(F32) * freq[...]
    cos = jnp.cos(angle)
    sin = jnp.sin(angle)
    sin = jnp.where(lane < HEAD_DIM // 2, -sin, sin)
    q_gain = qgain[...].astype(F32).reshape(1, HEAD_DIM) * QSCALE
    k_gain = kgain[...].astype(F32).reshape(1, HEAD_DIM)

    def send_queries(half):
        rows = slice(half * HALF, (half + 1) * HALF)
        turned = rotated(normed(pre[rows, :], q_gain), cos[rows], sin[rows]).astype(BF16)
        q_all[half][my_c] = turned

        def send_q(n, carry):
            dest = neighbour(my_x ^ pick(FAR_FIRST, n >> J_BITS), n & (JJ - 1))
            remote(
                q_all[half].at[my_c], q_all[half].at[my_c], qs_sem.at[half], qr_sem.at[half], ctx=dest
            ).start()
            return carry

        lax.fori_loop(0, C - 1, send_q, 0)
        drains.append(lambda: bytes_of(q_all[half].at[pl.ds(0, C - 1)], qs_sem.at[half]))
        return turned

    for r in range(STAY):
        pre[r * Q : (r + 1) * Q, :] = raw[order[r], :Q, :]
        kv_pre[r * STEPS : (r + 1) * STEPS, :] = raw[order[r], Q : Q + STEPS, :]
    queries = [send_queries(0)]

    ALL = JJ * HALF
    at, to = iota((ALL, ALL), 0), iota((ALL, ALL), 1)
    to_rows = to == ((at >> 2) & (JJ - 1)) * HALF + (at >> (2 + J_BITS)) * Q + (at & 3)
    to_devices = to == ((at >> 2) & 3) * (JJ * Q) + (at >> 4) * Q + (at & 3)
    to_rows = to_rows.astype(F32).astype(BF16)
    to_devices = to_devices.astype(F32).astype(BF16)
    gather = iota((JJ, 2 * ALL), 0) == ((iota((JJ, 2 * ALL), 1) >> 2) & (JJ - 1))
    gather = gather.astype(F32).astype(BF16)

    bytes_of(z_recv, zr_sem)
    for n in range(1, G):
        r = STAY + n - 1
        pre[r * Q : (r + 1) * Q, :] = z_recv[G - 1 - n, :Q, :]
        kv_pre[r * STEPS : (r + 1) * STEPS, :] = z_recv[G - 1 - n, Q : Q + STEPS, :]
    queries.append(send_queries(1))

    kv_send[...] = kv_pre[...].astype(BF16)
    kv_bits = PIECES.bit_length() - 1
    kv_head = (my_c & (C // 2 - 1)) >> kv_bits
    kv_slot = ((my_c >> (C.bit_length() - 2)) << kv_bits) + (my_c & (PIECES - 1))

    def send_kv(n, carry):
        dest = kv_head * JJ + n

        @pl.when(dest != my_c)
        def _():
            remote(kv_send, kv_recv.at[kv_slot], ks_sem, kr_sem, ctx=dest).start()

        return carry

    lax.fori_loop(0, JJ, send_kv, 0)

    @pl.when(kv_head == my_x)
    def _():
        kv_recv[kv_slot] = kv_send[...]

    def drain_kv():
        @pl.when(kv_head == my_x)
        def _():
            if JJ > 1:
                bytes_of(kv_recv.at[pl.ds(0, JJ - 1)], ks_sem)

        @pl.when(kv_head != my_x)
        def _():
            bytes_of(kv_recv.at[pl.ds(0, JJ)], ks_sem)

    drains.append(drain_kv)

    M = JJ * Q
    place = iota((2 * M, BLK), 1) + my_c * BLK
    lanes = iota((2 * M, HEAD_DIM), 1) - (iota((2 * M, HEAD_DIM), 0) & 3)
    loads[-2].wait()

    PAIR = 2 * HEAD_DIM
    unit = (iota((PAIR, PAIR), 0) == iota((PAIR, PAIR), 1)).astype(F32).astype(BF16)
    for n, r in enumerate(halves[1]):
        for k in range(KV_HEADS // 2):
            at = slice(k * PAIR, (k + 1) * PAIR)
            x = lax.dot_general(
                unit, cache[order[r], :, at], (((1,), (1,)), ((), ())), preferred_element_type=F32
            )
            turned_keys[n, at, :] = x.astype(BF16)

    def attend(half):
        rows = halves[half]
        send, recv = a_send.at[half], a_recv.at[half]

        bytes_of(q_all[half].at[pl.ds(0, C - 1)], qr_sem.at[half])

        def two_planes(i):
            first = (my_x & 2) ^ (2 - 2 * i)
            nearer = my_x ^ (3 - 2 * i)
            last = my_x ^ (2 - 2 * i)
            k_at = pl.ds(pl.multiple_of(first * HEAD_DIM, 2 * HEAD_DIM), 2 * HEAD_DIM)
            v_at = pl.ds(pl.multiple_of((first + KV_HEADS) * HEAD_DIM, 2 * HEAD_DIM), 2 * HEAD_DIM)
            came = [q_all[half][pl.ds((first + m) * JJ, JJ)].reshape(ALL, HEAD_DIM) for m in range(2)]
            came = [jnp.dot(to_rows, x, preferred_element_type=F32).astype(BF16) for x in came]
            blank = jnp.zeros((M, HEAD_DIM), BF16)
            scores, peaks, weights, totals, sums, high, low = [], [], [], [], [], [], []
            for n, r in enumerate(rows):
                a, b = [x[n * M : (n + 1) * M] for x in came]
                both = jnp.concatenate(
                    [jnp.concatenate([a, blank], axis=1), jnp.concatenate([blank, b], axis=1)], axis=0
                )
                if half:
                    x = jnp.dot(both, turned_keys[n, k_at, :], preferred_element_type=F32)
                else:
                    x = lax.dot_general(
                        both, cache[order[r], :, k_at], (((1,), (1,)), ((), ())), preferred_element_type=F32
                    )
                scores.append(jnp.where(place < row_lengths[r], x, FLOOR))
            for x in scores:
                peaks.append(jnp.maximum(jnp.max(x, axis=1, keepdims=True), LOW).astype(BF16).astype(F32))
            for x, peak in zip(scores, peaks):
                x = jnp.exp2(x - peak)
                totals.append(jnp.sum(x, axis=1, keepdims=True))
                weights.append(x.astype(BF16))
            for x, r in zip(weights, rows):
                sums.append(jnp.dot(x, cache[order[r], :, v_at], preferred_element_type=F32).astype(BF16))
            for n, (peak, total) in enumerate(zip(peaks, totals)):
                rounded = total.astype(BF16).astype(F32)
                n = rows[n] * Q
                x = jnp.where(lanes == n, peak, jnp.where(lanes == RQ + n, rounded, 0.0))
                high.append(x.astype(BF16))
                low.append(jnp.where(lanes == RQ + n, total - rounded, 0.0).astype(BF16))
            for m in range(2):
                mine = slice(m * M, (m + 1) * M)
                x = jnp.concatenate([x[mine, m * HEAD_DIM : (m + 1) * HEAD_DIM] for x in sums], axis=0)
                x = jnp.dot(to_devices, x, preferred_element_type=F32)
                send[pl.ds((first + m) * JJ, JJ)] = x.astype(BF16).reshape(JJ, HALF, HEAD_DIM)
                x = jnp.concatenate([x[mine] for x in high + low], axis=0)
                x = jnp.dot(gather, x, preferred_element_type=F32)
                if half:
                    x = x + ml_send[pl.ds((first + m) * JJ, JJ), 0, :]
                ml_send[pl.ds((first + m) * JJ, JJ), 0, :] = x

            def send_to(n, carry):
                dest = neighbour(jnp.where((n >= JJ) == (i == 1), last, nearer), n & (JJ - 1))
                if half:
                    remote(ml_send.at[dest], ml_recv.at[my_c], ms_sem, mr_sem, ctx=dest).start()
                remote(send.at[dest], recv.at[my_c], as_sem, ar_sem, ctx=dest).start()

                return carry

            if half:
                turns = range(2 * JJ - i)
                if JJ == 8:
                    turns = (0, 1, 8, 9, 2, 3, 4, 5, 10, 11, 12, 13, 6, 7, 14, 15)[: 2 * JJ - i]
                for n in turns:
                    send_to(n, 0)
            else:
                lax.fori_loop(0, 2 * JJ - i, send_to, 0)

        two_planes(0)
        two_planes(1)
        recv[my_c] = send[my_c]

    attend(0)
    attend(1)
    ml_recv[my_c] = ml_send[my_c]
    drains.append(lambda: bytes_of(a_send.at[:, pl.ds(0, C - 1)], as_sem))
    drains.append(lambda: bytes_of(ml_send.at[pl.ds(0, C - 1)], ms_sem))

    @pl.when(kv_head == my_x)
    def _():
        bytes_of(kv_recv.at[pl.ds(0, 2 * PIECES - 1)], kr_sem)

    @pl.when(kv_head != my_x)
    def _():
        bytes_of(kv_recv.at[pl.ds(0, 2 * PIECES)], kr_sem)

    new = []
    piece = iota((SR, HEAD_DIM), 1) >> (KVW.bit_length() - 1)
    for kind in range(2):
        x = kv_recv[kind * PIECES].astype(F32)
        for n in range(1, PIECES):
            x = jnp.where(piece == n, kv_recv[kind * PIECES + n].astype(F32), x)
        new.append(x)
    new_key = rotated(normed(new[0], k_gain), cos[RQ:], sin[RQ:]).astype(BF16)
    new_value = new[1].astype(BF16)
    q_mine = jnp.concatenate(queries, axis=0)
    scores = lax.dot_general(q_mine, new_key, (((1,), (1,)), ((), ())), preferred_element_type=F32)
    ti, tj = iota(scores.shape, 0), iota(scores.shape, 1)
    scores = jnp.where(((ti >> 2) == (tj >> 1)) & ((tj & 1) <= (ti & 1)), scores, FLOOR)
    new_peak = jnp.max(scores, axis=1, keepdims=True)
    weights = jnp.exp2(scores - new_peak)
    new_total = jnp.sum(weights, axis=1, keepdims=True)
    new_sums = jnp.dot(weights.astype(BF16), new_value, preferred_element_type=F32)

    bytes_of(ml_recv.at[pl.ds(0, C - 1)], mr_sem)
    stats = jnp.transpose(ml_recv[:, 0, :])
    peaks, totals = stats[:RQ], stats[RQ : 2 * RQ]
    highest = jnp.maximum(jnp.max(peaks, axis=1, keepdims=True), new_peak)
    scale = jnp.exp2(peaks - highest)
    new_scale = jnp.exp2(new_peak - highest)
    norm = jnp.sum(scale * totals, axis=1, keepdims=True) + new_scale * new_total
    for n in range(C):
        spread[n] = jnp.broadcast_to(scale[:, n : n + 1], (RQ, HEAD_DIM))
    bytes_of(a_recv.at[:, pl.ds(0, C - 1)], ar_sem)
    for half in range(2):
        rows = slice(half * HALF, (half + 1) * HALF)
        acc = [(new_sums * new_scale)[rows]] + [jnp.zeros((HALF, HEAD_DIM), F32)] * 3
        for n in range(C):
            acc[n & 3] = acc[n & 3] + a_recv[half, n].astype(F32) * spread[n, rows, :]
        mix[rows, :] = ((acc[0] + acc[1]) + (acc[2] + acc[3])) / norm[rows]
    mixed = jnp.concatenate(
        [
            jnp.concatenate([mix[pl.ds(j * STEPS + s, ROWS, stride=Q), :] for s in range(STEPS)], axis=0)
            for j in range(LOCAL_HEADS)
        ],
        axis=1,
    ).astype(BF16)

    loads[-1].wait()
    quarter = D // KV_HEADS
    width = D // C

    for i in range(KV_HEADS):
        g = my_x ^ FAR_FIRST[i]
        part = jnp.dot(
            mixed, wo[:, pl.ds(pl.multiple_of(g * quarter, quarter), quarter)], preferred_element_type=F32
        ).astype(BF16)
        for n in range(JJ):
            o_send[g * JJ + n] = part[:, n * width : (n + 1) * width]
        if i == 1:
            turns = [(0, n) for n in range(JJ)] + [(1, n) for n in range(JJ)]
        elif i == 3:
            turns = [(2, n) for n in range(JJ)] + [(3, n) for n in range(JJ - 1)]
            if JJ == 8:
                turns = [turns[n] for n in (0, 1, 8, 9, 2, 3, 4, 5, 10, 11, 12, 13, 6, 7, 14)]
        else:
            turns = []
        for a, n in turns:
            dest = neighbour(my_x ^ FAR_FIRST[a], n)
            remote(o_send.at[dest], o_recv.at[my_c], os_sem, or_sem, ctx=dest).start()
    drains.append(lambda: bytes_of(o_send.at[pl.ds(0, C - 1)], os_sem))
    o_recv[my_c] = o_send[my_c]
    bytes_of(o_recv.at[pl.ds(0, C - 1)], or_sem)
    result = jnp.sum(o_recv[...].astype(F32), axis=0)

    for n in range(G - 1):
        for s in range(STEPS):
            y_send[n, s : s + 1, :] = result[s * ROWS + STAY + n : s * ROWS + STAY + n + 1]
        y_send[n, STEPS:, :] = jnp.zeros((8 - STEPS, HEAD_DIM), F32)
    for n in range(G - 1):
        remote(y_send.at[n], y_recv.at[n], ys_sem, yr_sem, group=(my_g + n + 1) & (G - 1)).start()

    for drain in drains:
        drain()

    slot = iota((ROWS, HEAD_DIM), 0)
    lines = [jnp.zeros((ROWS, HEAD_DIM), F32)] * STEPS
    for s in range(STEPS):
        for r in range(STAY):
            lines[s] = jnp.where(slot == order[r], result[s * ROWS + r : s * ROWS + r + 1], lines[s])
    bytes_of(y_recv, yr_sem)
    for n in range(G - 1):
        for s in range(STEPS):
            lines[s] = jnp.where(slot == home[G - 1 - n], y_recv[n, s : s + 1, :], lines[s])
    bytes_of(y_send, ys_sem)
    for s in range(STEPS):
        out_ref[s] = lines[s].astype(BF16)


def per_device(G, C, hidden, cache, lengths, source, target, wq, wkv, qgain, kgain, wo):
    D = hidden.shape[-1]
    BLK = cache.shape[1]
    JJ = C // KV_HEADS
    pieces = C // 8
    half = np.arange(HEAD_DIM // 2, dtype=np.float64)
    freq = (THETA ** (-2.0 * half / HEAD_DIM)).astype(np.float32)
    freq = jnp.asarray(np.concatenate([freq, freq])[None])
    vmem = lambda x: pltpu.VMEM(x.shape, x.dtype)
    smem = lambda x: pltpu.SMEM(x.shape, x.dtype)
    dma = pltpu.SemaphoreType.DMA
    wkv = wkv.T
    operands = (hidden, cache, lengths, source, target, wq, wkv, qgain, kgain, wo, freq)
    return pl.pallas_call(
        functools.partial(kernel, G, C, D, BLK),
        out_shape=jax.ShapeDtypeStruct((STEPS, ROWS, D // C), BF16),
        in_specs=[pl.BlockSpec(memory_space=pltpu.HBM)] * len(operands),
        out_specs=pl.BlockSpec(memory_space=pltpu.VMEM),
        scratch_shapes=[
            vmem(hidden), vmem(cache), vmem(wq), vmem(wkv), vmem(wo), vmem(qgain), vmem(kgain), vmem(freq),
            smem(lengths), smem(source), smem(target),
            pltpu.VMEM((ROWS, 8, HEAD_DIM), F32),
            pltpu.VMEM((G - 1, 8, HEAD_DIM), F32),
            pltpu.VMEM((G - 1, 8, HEAD_DIM), F32),
            pltpu.VMEM((RQ, HEAD_DIM), F32),
            pltpu.VMEM((C, HALF, HEAD_DIM), BF16),
            pltpu.VMEM((C, HALF, HEAD_DIM), BF16),
            pltpu.VMEM((ROWS // 2, KV_HEADS * HEAD_DIM, BLK), BF16),
            pltpu.VMEM((SR, HEAD_DIM), F32),
            pltpu.VMEM((SR, HEAD_DIM), BF16),
            pltpu.VMEM((max(2 * pieces, JJ), SR, HEAD_DIM), BF16),
            pltpu.VMEM((2, C, HALF, HEAD_DIM), BF16),
            pltpu.VMEM((2, C, HALF, HEAD_DIM), BF16),
            pltpu.VMEM((C, 1, HEAD_DIM), F32),
            pltpu.VMEM((C, 1, HEAD_DIM), F32),
            pltpu.VMEM((C, RQ, HEAD_DIM), F32),
            pltpu.VMEM((RQ, HEAD_DIM), F32),
            pltpu.VMEM((C, SR, D // C), BF16),
            pltpu.VMEM((C, SR, D // C), BF16),
            pltpu.VMEM((G - 1, 8, HEAD_DIM), F32),
            pltpu.VMEM((G - 1, 8, HEAD_DIM), F32),
            dma((11,)), dma, dma, dma((2,)), dma((2,)), dma, dma, dma, dma, dma, dma, dma, dma, dma, dma,
        ],
        compiler_params=pltpu.CompilerParams(
            collective_id=0, has_side_effects=True, vmem_limit_bytes=62 * 1024 * 1024
        ),
    )(*operands)


def solution(mesh):
    in_specs = (
        P(None, "group", None),
        P("group", "ctx", None),
        P(),
        P(),
        P(),
        P(None, "ctx"),
        P(None, "ctx"),
        P(),
        P(),
        P("ctx", None),
    )
    return jax.shard_map(
        functools.partial(per_device, mesh.shape["group"], mesh.shape["ctx"]),
        mesh=mesh, in_specs=in_specs, out_specs=P(None, "group", "ctx"), check_vma=False,
    )
```
